32 devices in a mesh: chan: 8 (over z, x), win: 4 (over y, core).
Axes of the slice: x: 2, y: 2, z: 4, core: 2. Of those that a mesh axis runs over, the one named last changes fastest.
Arguments:
- records: bfloat16 [10240, 102400], P('chan', 'win'), may hold values from -6 to 6
- offsets: int32 [32], P('win'), may hold values from 0 to 128
- src_index: int32 [4, 4], replicated, may hold values from 0 to 10239, as said below
- quality: int32 [10240], P('chan'), may hold values 0 or 1
Outputs:
- stacks: float32 [4, 196, 10240], P('win', None, 'chan')
The draws below stay inside these ranges and needn't reach their ends.
Inputs may be any that keep to these rules, and one draw needn't show every extreme that they name: `src_index`: the 4 channels of one step are distinct and lie in one aligned block of 1280 channels; some step includes channel 0 and some other step the last channel.
All inputs are finite; a program needn't handle non-finite values. No bound on the sum of `quality` on one device may be relied on, other than what follows from the above.
Results may differ from the reference program's by a relative error of at most 0.0038.
Values may be sent and summed in bfloat16 or wider, within the bound.
No kernel may reach another device: no remote copies, remote signals or barrier semaphores. Data moves between devices by JAX's collectives and lax.ppermute only.
A program may use at most 320 MiB of HBM per device.

```python
import math
import jax
import jax.numpy as jnp
from jax import lax

C = 10240
L = 3072
LAGS = 49
NSRC = 4
STEPS = 4
GAP = 128
STRIDE = 3200
SEGMENTS = 32
SAMPLES = 102400
CH_DEV = 1280


def draw_src_index(key, part):
    key_owner = jax.random.fold_in(key, 11)
    key_local = jax.random.fold_in(key, 12)
    key_pick = jax.random.fold_in(key, 13)
    key_other = jax.random.fold_in(key, 14)
    key_high = jax.random.fold_in(key, 15)
    key_low = jax.random.fold_in(key, 16)
    owner = jax.random.randint(key_owner, (STEPS, 1), 0, C // CH_DEV)
    chosen = jnp.stack([jax.random.permutation(jax.random.fold_in(key_local, number), CH_DEV)[:NSRC] for number in range(STEPS)])
    high_row = jnp.concatenate([jax.random.permutation(key_high, CH_DEV - 1)[:NSRC - 1], jnp.full((1,), CH_DEV - 1, jnp.int32)])
    low_row = jnp.concatenate([jnp.zeros((1,), jnp.int32), 1 + jax.random.permutation(key_low, CH_DEV - 1)[:NSRC - 1]])
    first = jax.random.randint(key_pick, (), 0, STEPS)
    second = (first + 1 + jax.random.randint(key_other, (), 0, STEPS - 1)) % STEPS
    rows = jnp.arange(STEPS, dtype=jnp.int32)[:, None]
    chosen = jnp.where(rows == first, high_row[None, :], jnp.where(rows == second, low_row[None, :], chosen))
    owner = jnp.where(rows == first, C // CH_DEV - 1, jnp.where(rows == second, 0, owner))
    return (owner * CH_DEV + chosen).astype(jnp.int32)


def draw_offsets(key, part):
    key_value = jax.random.fold_in(key, 21)
    key_first = jax.random.fold_in(key, 22)
    key_second = jax.random.fold_in(key, 23)
    values = jax.random.randint(key_value, (SEGMENTS,), 0, GAP + 1)
    first = jax.random.randint(key_first, (), 0, SEGMENTS)
    second = (first + 1 + jax.random.randint(key_second, (), 0, SEGMENTS - 1)) % SEGMENTS
    values = values.at[first].set(GAP).at[second].set(0)
    return values.astype(jnp.int32)


def touch_ends(values, stream_key, least, largest):
    place = [jax.random.randint(jax.random.fold_in(stream_key, axis), (), 0, length) for axis, length in enumerate(values.shape)]
    widest = values.shape.index(max(values.shape))
    neighbour = place[:widest] + [(place[widest] + 1) % values.shape[widest]] + place[widest + 1:]
    return values.at[tuple(place)].set(least).at[tuple(neighbour)].set(largest)


def levels(rng, dims, split, low, largest):
    gain, own = 1.0, jax.random.fold_in(rng, 6)
    for axis_at, shards_of in split:
        draws = jnp.exp(jax.random.uniform(jax.random.fold_in(own, axis_at), (shards_of,), jnp.float32, low / len(split), largest / len(split)))
        gain = gain * jnp.repeat(draws, dims[axis_at] // shards_of).reshape([-1 if axis == axis_at else 1 for axis in range(len(dims))])
    return gain


def bell_draw(stream_key, shape, width, reach, split=(), kind=jnp.bfloat16):
    array = jax.random.normal(stream_key, shape, jnp.float32) * width
    if len(split) > 0:
        array = levels(stream_key, shape, split, -0.22, 0.18) * array
    return jnp.clip(array, min=-reach, max=reach).astype(kind)


def setup_inputs(seed: int = 0) -> dict:
    splits = jax.random.split(jax.random.key(seed), 5)
    return {
        "records": bell_draw(splits[0], (C, SAMPLES), 1.0, 6.0, ((0, 8), (1, 4))),
        "offsets": draw_offsets(jax.random.fold_in(splits[4], 71), 0),
        "src_index": draw_src_index(jax.random.fold_in(splits[4], 71), 0),
        "quality": touch_ends((jax.random.randint(splits[3], (C,), 0, 8) < 7).astype(jnp.int32), jax.random.fold_in(splits[3], 1), 0, 1),
    }


EPSILON = 1e-06

def whiten(segment):
    values = segment.astype(jnp.float32)
    power = lax.optimization_barrier(jnp.mean(values * values, axis=-1, keepdims=True))
    return (values / jnp.sqrt(power + EPSILON)).astype(jnp.bfloat16)

def lagged(source):
    half = (LAGS - 1) // 2
    length = source.shape[-1]
    widths = [(0, 0)] * (source.ndim - 1) + [(half, half)]
    padded = jnp.pad(source, widths)
    return jnp.stack([padded[..., 2 * half - column:2 * half - column + length] for column in range(LAGS)], axis=-2)

def reference(records, offsets, src_index, quality):
    starts = jnp.arange(SEGMENTS, dtype=jnp.int32) * STRIDE + offsets.astype(jnp.int32)

    def accumulate(total, begin):
        segment = lax.dynamic_slice_in_dim(records, begin, L, 1)
        white = whiten(segment)
        sources = white[src_index]
        shifted = lagged(sources).reshape(STEPS, NSRC * LAGS, L)
        term = jnp.einsum('kpt,ct->kpc', shifted.astype(jnp.float32), white.astype(jnp.float32), precision=lax.Precision.HIGHEST)
        return (total + term, None)
    initial = jnp.zeros((STEPS, NSRC * LAGS, C), jnp.float32)
    total, _ = lax.scan(accumulate, initial, starts)
    scale = 1.0 / math.sqrt(SEGMENTS * L)
    return total * scale * quality.astype(jnp.float32)[None, None, :]
```

```python
import functools
import math

import jax
import jax.numpy as jnp
from jax import lax
from jax.experimental import pallas as pl
from jax.experimental.pallas import tpu as pltpu
from jax.sharding import PartitionSpec as P

L = 3072
LAGS = 49
HALF = (LAGS - 1) // 2
EVEN = HALF + 1
ODD = HALF
EPSILON = 1e-06
LANES = 128
TILES = L // LANES
PAIRS = TILES // 2
ROWS = 64
COLUMNS = 256


def lanes(rows, dtype=jnp.int32):
    return lax.broadcasted_iota(dtype, (rows, LANES), 1)


def source_kernel(offsets_ref, rows_ref, own_ref, out_ref):
    count = rows_ref.shape[0]
    seg_count = out_ref.shape[0]
    stride = rows_ref.shape[1] // seg_count
    lane = lanes(count)
    owned = own_ref[...] > 0

    def one(g, carry):
        off = offsets_ref[g]
        back = lax.rem(LANES - off, LANES)
        base = g * stride
        tiles = []
        for m in range(TILES + 1):
            start = pl.multiple_of(base + m * LANES, LANES)
            tiles.append(rows_ref[:, pl.ds(start, LANES)].astype(jnp.float32))
        cut = [jnp.where(lane < off, tiles[m + 1], tiles[m]) for m in range(TILES)]
        total = cut[0] * cut[0]
        for m in range(1, TILES):
            total = total + cut[m] * cut[m]
        power = jnp.sum(total, axis=1, keepdims=True) / L
        root = jnp.sqrt(power + EPSILON)
        for m in range(TILES):
            white = jnp.where(owned, pltpu.roll(cut[m], back, 1) / root, 0.0)
            out_ref[g, :, m * LANES : (m + 1) * LANES] = white.astype(jnp.bfloat16)
        return carry

    lax.fori_loop(0, seg_count, one, 0)


def phases(u_ref, seg, count):
    lane = lanes(count)
    even = lane % 2 == 0
    zero = jnp.zeros((count, LANES), jnp.float32)

    def tile(m):
        if m < 0 or m >= TILES:
            return zero
        return u_ref[seg, :, m * LANES : (m + 1) * LANES].astype(jnp.float32)

    plain, ahead, behind = [], [], []
    for p in range(-1, PAIRS + 1):
        low, high, before = tile(2 * p), tile(2 * p + 1), tile(2 * p - 1)
        low_on = pltpu.roll(low, 1, 1)
        high_on = pltpu.roll(high, 1, 1)
        before_on = pltpu.roll(before, 1, 1)
        plain.append(jnp.where(even, low, high_on))
        ahead.append(jnp.where(even, pltpu.roll(low, LANES - 1, 1) - low, high - high_on))
        late_low = jnp.where(lane == 0, before_on, low_on)
        late_high = jnp.where(lane == 0, low_on, high_on)
        behind.append(jnp.where(even, late_low - low, pltpu.roll(late_high, 1, 1) - high_on))
    return plain, ahead, behind


def build(tiles, lag_count, off, a_ref, count):
    lane = lanes(count)
    even = lane % 2 == 0
    shifted = []
    for p in range(PAIRS + 1):
        back = pltpu.roll(tiles[p], LANES - 1, 1)
        on = pltpu.roll(tiles[p + 1], 1, 1)
        shifted.append(jnp.where(even, back, on))
    now = jnp.concatenate(tiles[1 : PAIRS + 1], axis=0)
    early = jnp.concatenate(shifted[:PAIRS], axis=0)
    late = jnp.concatenate(shifted[1:], axis=0)
    wide = lanes(count * PAIRS)
    for index in range(lag_count):
        s = 2 * index - HALF
        if s > 0:
            z = jnp.where(wide >= LANES - s, early, now)
        elif s < 0:
            z = jnp.where(wide < -s, late, now)
        else:
            z = now
        z = pltpu.roll(z, lax.rem(off + (s + LANES), LANES), 1).astype(jnp.bfloat16)
        for p in range(PAIRS):
            a_ref[index * count : (index + 1) * count, p * LANES : (p + 1) * LANES] = z[
                p * count : (p + 1) * count
            ]


def prepare(x_ref, off, row, w_refs, at, sum_ref):
    lane = lanes(ROWS)
    early = lane < off
    even = lax.rem(lane + (LANES - off) % 2, 2) == 0
    total = jnp.zeros((ROWS, LANES), jnp.float32)
    first_ref, second_ref, both_ref = w_refs

    def tile(m):
        return x_ref[row : row + ROWS, m * LANES : (m + 1) * LANES]

    for p in range(PAIRS):
        a, b, c = tile(2 * p), tile(2 * p + 1), tile(2 * p + 2)
        low = jnp.where(early, b, a).astype(jnp.float32)
        high = jnp.where(early, c, b).astype(jnp.float32)
        total = total + low * low + high * high
        first = jnp.where(even, low, pltpu.roll(high, 1, 1))
        second = jnp.where(even, pltpu.roll(low, LANES - 1, 1), high)
        span = slice(p * LANES, (p + 1) * LANES)
        first_ref[at : at + ROWS, span] = first.astype(jnp.bfloat16)
        second_ref[at : at + ROWS, span] = second.astype(jnp.bfloat16)
        both_ref[at : at + ROWS, span] = (first + second).astype(jnp.bfloat16)
    sum_ref[at : at + ROWS, :] = total


def dot(a, b):
    return lax.dot_general(a, b, (((1,), (1,)), ((), ())), preferred_element_type=jnp.float32)


def stack_kernel(
    src_count, offsets_ref, win_ref, u_ref, x_ref, keep_ref, send_ref,
    a1, a2, a3, c1, c2, c3, w00, w01, w02, w10, w11, w12, s0, s1, stage,
):
    g = pl.program_id(0)
    last = pl.num_programs(0) - 1
    off = offsets_ref[g]
    channels = x_ref.shape[0]
    count = u_ref.shape[1]
    slots = (((w00, w01, w02), s0), ((w10, w11, w12), s1))
    blocks = [(c, min(COLUMNS, channels - c)) for c in range(0, channels, COLUMNS)]

    @pl.when(g == 0)
    def _():
        for c in (c1, c2, c3):
            c[...] = jnp.zeros_like(c)

    plain, ahead, behind = phases(u_ref, g, count)
    build(plain, EVEN, off, a1, count)
    build(ahead, EVEN, off, a2, count)
    build(behind, ODD, off, a3, count)

    def pieces(number):
        start, width = blocks[number]
        w_refs, sum_ref = slots[number % 2]
        return [
            functools.partial(prepare, x_ref, off, start + at, w_refs, at, sum_ref)
            for at in range(0, width, ROWS)
        ]

    for piece in pieces(0):
        piece()
    for number, (start, width) in enumerate(blocks):
        todo = pieces(number + 1) if number + 1 < len(blocks) else []
        (first, second, both), sum_ref = slots[number % 2]
        power = jnp.sum(jnp.transpose(sum_ref[:width, :]), axis=0, keepdims=True) / L
        gain = lax.rsqrt(power + EPSILON)
        for a, w, c in ((a1, both, c1), (a2, second, c2), (a3, first, c3)):
            term = dot(a[...], w[:width, :]) * gain
            for at in range(0, width, LANES):
                size = min(LANES, width - at)
                c[(start + at) // LANES, :, :size] += term[:, at : at + size]
            for piece in todo[:2]:
                piece()
            todo = todo[2:]

    @pl.when(g == last)
    def _():
        c2[...] += c1[...]
        c3[...] += c1[:, : ODD * count, :]
        for slot in range(4):
            step = win_ref[0] ^ slot
            out = send_ref if slot % 2 else keep_ref
            for start in range(0, channels, LANES):
                width = min(LANES, channels - start)
                evens, odds = c2.at[start // LANES], c3.at[start // LANES]
                for i in range(src_count):
                    row = step * src_count + i
                    here = i * LAGS
                    stage[pl.ds(here, EVEN, stride=2), :] = evens[pl.ds(row, EVEN, stride=count), :]
                    stage[pl.ds(here + 1, ODD, stride=2), :] = odds[pl.ds(row, ODD, stride=count), :]
                out[slot // 2, :, start : start + width] = stage[:, :width]


def exchange(value, axis, size):
    me = lax.axis_index(axis)

    def swap(v, bit):
        return lax.ppermute(v, axis, [(d, d ^ bit) for d in range(size)])

    half = value.shape[0] // 2
    low = me % 2 == 0
    one, two = value[:half], value[half:]
    mine = jnp.where(low, one, two) + swap(jnp.where(low, two, one), 1)
    bit = 2
    while bit < size:
        mine = mine + swap(mine, bit)
        bit *= 2
    other = swap(mine, 1)
    return jnp.concatenate([jnp.where(low, mine, other), jnp.where(low, other, mine)], axis=0)


def solution(mesh):
    chan = mesh.shape["chan"]
    win = mesh.shape["win"]

    def body(records, offsets, src_index, quality):
        channels, samples = records.shape
        seg_count = offsets.shape[0]
        stride = samples // seg_count
        step_count, src_count = src_index.shape
        count = step_count * src_count
        flat = src_index.reshape(-1)
        own = (flat // channels == lax.axis_index("chan")).astype(jnp.int32)[:, None]
        rows = jnp.take(records, flat % channels, axis=0)
        smem = pl.BlockSpec(memory_space=pltpu.SMEM)
        vmem = pl.BlockSpec(memory_space=pltpu.VMEM)
        sources = pl.pallas_call(
            source_kernel,
            out_shape=jax.ShapeDtypeStruct((seg_count, count, L), jnp.bfloat16),
            in_specs=[smem, vmem, vmem],
            out_specs=vmem,
            compiler_params=pltpu.CompilerParams(vmem_limit_bytes=32 * 2**20),
            name="sources",
        )(offsets, rows, own)
        sources = exchange(sources, "chan", chan)

        w = lax.axis_index("win").astype(jnp.int32).reshape(1)
        half = jax.ShapeDtypeStruct((2, src_count * LAGS, channels), jnp.float32)
        bf16 = functools.partial(pltpu.VMEM, dtype=jnp.bfloat16)
        f32 = functools.partial(pltpu.VMEM, dtype=jnp.float32)
        depth = L // 2
        groups = pl.cdiv(channels, LANES)
        keep, send = pl.pallas_call(
            functools.partial(stack_kernel, src_count),
            grid=(seg_count,),
            out_shape=(half, half),
            in_specs=[smem, smem, vmem, pl.BlockSpec((channels, stride), lambda g: (0, g))],
            out_specs=(vmem, vmem),
            scratch_shapes=[
                bf16((EVEN * count, depth)),
                bf16((EVEN * count, depth)),
                bf16((ODD * count, depth)),
                f32((groups, EVEN * count, LANES)),
                f32((groups, EVEN * count, LANES)),
                f32((groups, ODD * count, LANES)),
            ]
            + [bf16((COLUMNS, depth))] * 6
            + [f32((COLUMNS, LANES))] * 2
            + [f32((src_count * LAGS, LANES))],
            compiler_params=pltpu.CompilerParams(vmem_limit_bytes=56 * 2**20),
            cost_estimate=pl.CostEstimate(
                flops=2 * seg_count * (2 * EVEN + ODD) * count * depth * channels,
                bytes_accessed=records.size * 2,
                transcendentals=0,
            ),
            name="stacks",
        )(offsets, w, sources, records)

        def swap(v, bit):
            return lax.ppermute(v, "win", [(d, d ^ bit) for d in range(win)])

        pair = keep + swap(send, 1)
        total = pair[0] + swap(pair[1].astype(jnp.bfloat16), 2).astype(jnp.float32)
        scale = 1.0 / math.sqrt(seg_count * win * L)
        return (total * scale * quality.astype(jnp.float32)[None, :])[None]

    return jax.shard_map(
        body,
        mesh=mesh,
        in_specs=(P("chan", "win"), P("win"), P(), P("chan")),
        out_specs=P("win", None, "chan"),
        check_vma=False,
    )
```

```python
import functools
import math

import jax
import jax.numpy as jnp
from jax import lax
from jax.experimental import pallas as pl
from jax.experimental.pallas import tpu as pltpu
from jax.sharding import PartitionSpec as P

L = 3072
LAGS = 49
HALF = (LAGS - 1) // 2
EVEN = HALF + 1
ODD = HALF
EPSILON = 1e-06
LANES = 128
TILES = L // LANES
PAIRS = TILES // 2
ROWS = 64
COLUMNS = 512


def lanes(rows, dtype=jnp.int32):
    return lax.broadcasted_iota(dtype, (rows, LANES), 1)


def source_kernel(offsets_ref, rows_ref, own_ref, out_ref):
    count = rows_ref.shape[0]
    seg_count = out_ref.shape[0]
    stride = rows_ref.shape[1] // seg_count
    lane = lanes(count)
    owned = own_ref[...] > 0

    def one(g, carry):
        off = offsets_ref[g]
        back = lax.rem(LANES - off, LANES)
        base = g * stride
        tiles = []
        for m in range(TILES + 1):
            start = pl.multiple_of(base + m * LANES, LANES)
            tiles.append(rows_ref[:, pl.ds(start, LANES)].astype(jnp.float32))
        cut = [jnp.where(lane < off, tiles[m + 1], tiles[m]) for m in range(TILES)]
        total = cut[0] * cut[0]
        for m in range(1, TILES):
            total = total + cut[m] * cut[m]
        power = jnp.sum(total, axis=1, keepdims=True) / L
        root = jnp.sqrt(power + EPSILON)
        for m in range(TILES):
            white = jnp.where(owned, pltpu.roll(cut[m], back, 1) / root, 0.0)
            out_ref[g, :, m * LANES : (m + 1) * LANES] = white.astype(jnp.bfloat16)
        return carry

    lax.fori_loop(0, seg_count, one, 0)


def phases(u_ref, seg, count):
    lane = lanes(count)
    even = lane % 2 == 0
    zero = jnp.zeros((count, LANES), jnp.float32)

    def tile(m):
        if m < 0 or m >= TILES:
            return zero
        return u_ref[seg, :, m * LANES : (m + 1) * LANES].astype(jnp.float32)

    plain, ahead, behind = [], [], []
    for p in range(-1, PAIRS + 1):
        low, high, before = tile(2 * p), tile(2 * p + 1), tile(2 * p - 1)
        low_on = pltpu.roll(low, 1, 1)
        high_on = pltpu.roll(high, 1, 1)
        before_on = pltpu.roll(before, 1, 1)
        plain.append(jnp.where(even, low, high_on))
        ahead.append(jnp.where(even, pltpu.roll(low, LANES - 1, 1) - low, high - high_on))
        late_low = jnp.where(lane == 0, before_on, low_on)
        late_high = jnp.where(lane == 0, low_on, high_on)
        behind.append(jnp.where(even, late_low - low, pltpu.roll(late_high, 1, 1) - high_on))
    return plain, ahead, behind


def build(tiles, lag_count, off, a_ref, count):
    lane = lanes(count)
    even = lane % 2 == 0
    shifted = []
    for p in range(PAIRS + 1):
        back = pltpu.roll(tiles[p], LANES - 1, 1)
        on = pltpu.roll(tiles[p + 1], 1, 1)
        shifted.append(jnp.where(even, back, on))
    now = jnp.concatenate(tiles[1 : PAIRS + 1], axis=0).astype(jnp.bfloat16)
    early = jnp.concatenate(shifted[:PAIRS], axis=0).astype(jnp.bfloat16)
    late = jnp.concatenate(shifted[1:], axis=0).astype(jnp.bfloat16)
    wide = lanes(count * PAIRS)
    for index in range(lag_count):
        s = 2 * index - HALF
        if s > 0:
            z = jnp.where(wide >= LANES - s, early, now)
        elif s < 0:
            z = jnp.where(wide < -s, late, now)
        else:
            z = now
        z = pltpu.roll(z, lax.rem(off + (s + LANES), LANES), 1)
        for p in range(PAIRS):
            a_ref[index * count : (index + 1) * count, p * LANES : (p + 1) * LANES] = z[
                p * count : (p + 1) * count
            ]


def power_kernel(offsets_ref, x_ref, gain_ref):
    off = offsets_ref[pl.program_id(0)]
    channels = x_ref.shape[0]
    early = lanes(ROWS) < off
    for row in range(0, channels, LANES):
        sums = []
        for at in range(row, min(row + LANES, channels), ROWS):
            total = jnp.zeros((ROWS, LANES), jnp.float32)
            now = x_ref[at : at + ROWS, :LANES]
            for m in range(TILES):
                later = x_ref[at : at + ROWS, (m + 1) * LANES : (m + 2) * LANES]
                cut = jnp.where(early, later, now).astype(jnp.float32)
                total = total + cut * cut
                now = later
            sums.append(total)
        across = jnp.concatenate(sums, axis=0)
        power = jnp.sum(jnp.transpose(across), axis=0, keepdims=True) / L
        gain_ref[0, :, row : row + across.shape[0]] = lax.rsqrt(power + EPSILON)


def prepare(x_ref, off, row, w_refs, at):
    lane = lanes(ROWS)
    early = lane < off
    even = lax.rem(lane + off, 2) == 0
    first_ref, second_ref, both_ref = w_refs

    def tile(m):
        return x_ref[row : row + ROWS, m * LANES : (m + 1) * LANES]

    for p in range(PAIRS):
        a, b, c = tile(2 * p), tile(2 * p + 1), tile(2 * p + 2)
        low = jnp.where(early, b, a)
        high = jnp.where(early, c, b)
        first = jnp.where(even, low, pltpu.roll(high, 1, 1))
        second = jnp.where(even, pltpu.roll(low, LANES - 1, 1), high)
        span = slice(p * LANES, (p + 1) * LANES)
        first_ref[at : at + ROWS, span] = first
        second_ref[at : at + ROWS, span] = second
        both_ref[at : at + ROWS, span] = first + second


def dot(a, b):
    return lax.dot_general(a, b, (((1,), (1,)), ((), ())), preferred_element_type=jnp.float32)


def stack_kernel(
    src_count, offsets_ref, win_ref, u_ref, gain_ref, x_ref, keep_ref, send_ref,
    a1, a2, a3, c1, c2, c3, w00, w01, w02, w10, w11, w12, stage,
):
    g = pl.program_id(0)
    last = pl.num_programs(0) - 1
    off = offsets_ref[g]
    channels = x_ref.shape[0]
    count = u_ref.shape[1]
    slots = ((w00, w01, w02), (w10, w11, w12))
    blocks = [(c, min(COLUMNS, channels - c)) for c in range(0, channels, COLUMNS)]

    @pl.when(g == 0)
    def _():
        for c in (c1, c2, c3):
            c[...] = jnp.zeros_like(c)

    plain, ahead, behind = phases(u_ref, g, count)
    build(plain, EVEN, off, a1, count)
    build(ahead, EVEN, off, a2, count)
    build(behind, ODD, off, a3, count)

    def pieces(number):
        start, width = blocks[number]
        return [
            functools.partial(prepare, x_ref, off, start + at, slots[number % 2], at)
            for at in range(0, width, ROWS)
        ]

    for piece in pieces(0):
        piece()
    for number, (start, width) in enumerate(blocks):
        todo = pieces(number + 1) if number + 1 < len(blocks) else []
        first, second, both = slots[number % 2]
        gain = gain_ref[g, :, start : start + width]
        share = pl.cdiv(len(todo), 3)
        for a, w, c in ((a1, both, c1), (a2, second, c2), (a3, first, c3)):
            term = dot(a[...], w[:width, :]) * gain
            for at in range(0, width, LANES):
                size = min(LANES, width - at)
                c[(start + at) // LANES, :, :size] += term[:, at : at + size]
            for piece in todo[:share]:
                piece()
            todo = todo[share:]

    @pl.when(g == last)
    def _():
        c2[...] += c1[...]
        c3[...] += c1[:, : ODD * count, :]
        for slot in range(4):
            step = win_ref[0] ^ slot
            out = send_ref if slot % 2 else keep_ref
            for start in range(0, channels, LANES):
                width = min(LANES, channels - start)
                evens, odds = c2.at[start // LANES], c3.at[start // LANES]
                for i in range(src_count):
                    row = step * src_count + i
                    here = i * LAGS
                    stage[pl.ds(here, EVEN, stride=2), :] = evens[pl.ds(row, EVEN, stride=count), :]
                    stage[pl.ds(here + 1, ODD, stride=2), :] = odds[pl.ds(row, ODD, stride=count), :]
                out[slot // 2, :, start : start + width] = stage[:, :width]


def exchange(value, axis, size):
    me = lax.axis_index(axis)

    def swap(v, bit):
        return lax.ppermute(v, axis, [(d, d ^ bit) for d in range(size)])

    half = value.shape[0] // 2
    low = me % 2 == 0
    one, two = value[:half], value[half:]
    mine = jnp.where(low, one, two) + swap(jnp.where(low, two, one), 1)
    bit = 2
    while bit < size:
        mine = mine + swap(mine, bit)
        bit *= 2
    other = swap(mine, 1)
    return jnp.concatenate([jnp.where(low, mine, other), jnp.where(low, other, mine)], axis=0)


def solution(mesh):
    chan = mesh.shape["chan"]
    win = mesh.shape["win"]

    def body(records, offsets, src_index, quality):
        channels, samples = records.shape
        seg_count = offsets.shape[0]
        stride = samples // seg_count
        step_count, src_count = src_index.shape
        count = step_count * src_count
        flat = src_index.reshape(-1)
        own = (flat // channels == lax.axis_index("chan")).astype(jnp.int32)[:, None]
        rows = jnp.take(records, flat % channels, axis=0)
        smem = pl.BlockSpec(memory_space=pltpu.SMEM)
        vmem = pl.BlockSpec(memory_space=pltpu.VMEM)
        sources = pl.pallas_call(
            source_kernel,
            out_shape=jax.ShapeDtypeStruct((seg_count, count, L), jnp.bfloat16),
            in_specs=[smem, vmem, vmem],
            out_specs=vmem,
            compiler_params=pltpu.CompilerParams(vmem_limit_bytes=32 * 2**20),
            name="sources",
        )(offsets, rows, own)
        sources = exchange(sources, "chan", chan)
        segment = pl.BlockSpec((channels, stride), lambda g: (0, g))
        gain = pl.pallas_call(
            power_kernel,
            grid=(seg_count,),
            out_shape=jax.ShapeDtypeStruct((seg_count, 1, channels), jnp.float32),
            in_specs=[smem, segment],
            out_specs=pl.BlockSpec((1, 1, channels), lambda g: (g, 0, 0)),
            compiler_params=pltpu.CompilerParams(vmem_limit_bytes=32 * 2**20),
            cost_estimate=pl.CostEstimate(
                flops=2 * records.size, bytes_accessed=2 * records.size, transcendentals=0
            ),
            name="power",
        )(offsets, records)

        w = lax.axis_index("win").astype(jnp.int32).reshape(1)
        half = jax.ShapeDtypeStruct((2, src_count * LAGS, channels), jnp.float32)
        bf16 = functools.partial(pltpu.VMEM, dtype=jnp.bfloat16)
        f32 = functools.partial(pltpu.VMEM, dtype=jnp.float32)
        depth = L // 2
        groups = pl.cdiv(channels, LANES)
        keep, send = pl.pallas_call(
            functools.partial(stack_kernel, src_count),
            grid=(seg_count,),
            out_shape=(half, half),
            in_specs=[smem, smem, vmem, vmem, segment],
            out_specs=(vmem, vmem),
            scratch_shapes=[
                bf16((EVEN * count, depth)),
                bf16((EVEN * count, depth)),
                bf16((ODD * count, depth)),
                f32((groups, EVEN * count, LANES)),
                f32((groups, EVEN * count, LANES)),
                f32((groups, ODD * count, LANES)),
            ]
            + [bf16((COLUMNS, depth))] * 6
            + [f32((src_count * LAGS, LANES))],
            compiler_params=pltpu.CompilerParams(vmem_limit_bytes=56 * 2**20),
            cost_estimate=pl.CostEstimate(
                flops=2 * seg_count * (2 * EVEN + ODD) * count * depth * channels,
                bytes_accessed=records.size * 2,
                transcendentals=0,
            ),
            name="stacks",
        )(offsets, w, sources, gain, records)

        def swap(v, bit):
            return lax.ppermute(v, "win", [(d, d ^ bit) for d in range(win)])

        pair = keep + swap(send, 1)
        total = pair[0] + swap(pair[1].astype(jnp.bfloat16), 2).astype(jnp.float32)
        scale = 1.0 / math.sqrt(seg_count * win * L)
        return (total * scale * quality.astype(jnp.float32)[None, :])[None]

    return jax.shard_map(
        body,
        mesh=mesh,
        in_specs=(P("chan", "win"), P("win"), P(), P("chan")),
        out_specs=P("win", None, "chan"),
        check_vma=False,
    )
```

```python
import functools
import math

import jax
import jax.numpy as jnp
from jax import lax
from jax.experimental import pallas as pl
from jax.experimental.pallas import tpu as pltpu
from jax.sharding import PartitionSpec as P

L = 3072
LAGS = 49
HALF = (LAGS - 1) // 2
EVEN = HALF + 1
ODD = HALF
EPSILON = 1e-06
LANES = 128
TILES = L // LANES
PAIRS = TILES // 2
ROWS = 64
UNIT = 256


def lanes(rows, dtype=jnp.int32):
    return lax.broadcasted_iota(dtype, (rows, LANES), 1)


def source_kernel(offsets_ref, rows_ref, own_ref, out_ref):
    count = rows_ref.shape[0]
    seg_count = out_ref.shape[0]
    stride = rows_ref.shape[1] // seg_count
    lane = lanes(count)
    owned = own_ref[...] > 0

    def one(g, carry):
        off = offsets_ref[g]
        back = lax.rem(LANES - off, LANES)
        base = g * stride
        tiles = []
        for m in range(TILES + 1):
            start = pl.multiple_of(base + m * LANES, LANES)
            tiles.append(rows_ref[:, pl.ds(start, LANES)].astype(jnp.float32))
        cut = [jnp.where(lane < off, tiles[m + 1], tiles[m]) for m in range(TILES)]
        total = cut[0] * cut[0]
        for m in range(1, TILES):
            total = total + cut[m] * cut[m]
        power = jnp.sum(total, axis=1, keepdims=True) / L
        root = jnp.sqrt(power + EPSILON)
        for m in range(TILES):
            white = jnp.where(owned, pltpu.roll(cut[m], back, 1) / root, 0.0)
            out_ref[g, :, m * LANES : (m + 1) * LANES] = white.astype(jnp.bfloat16)
        return carry

    lax.fori_loop(0, seg_count, one, 0)


def phases(u_ref, seg, count):
    lane = lanes(count)
    even = lane % 2 == 0
    zero = jnp.zeros((count, LANES), jnp.float32)

    def tile(m):
        if m < 0 or m >= TILES:
            return zero
        return u_ref[seg, :, m * LANES : (m + 1) * LANES].astype(jnp.float32)

    plain, ahead, behind = [], [], []
    for p in range(-1, PAIRS + 1):
        low, high, before = tile(2 * p), tile(2 * p + 1), tile(2 * p - 1)
        low_on = pltpu.roll(low, 1, 1)
        high_on = pltpu.roll(high, 1, 1)
        before_on = pltpu.roll(before, 1, 1)
        plain.append(jnp.where(even, low, high_on))
        ahead.append(jnp.where(even, pltpu.roll(low, LANES - 1, 1) - low, high - high_on))
        late_low = jnp.where(lane == 0, before_on, low_on)
        late_high = jnp.where(lane == 0, low_on, high_on)
        behind.append(jnp.where(even, late_low - low, pltpu.roll(late_high, 1, 1) - high_on))
    return plain, ahead, behind


def builders(u_ref, seg, off, a_refs, count):
    lane = lanes(count)
    even = lane % 2 == 0
    wide = lanes(count * PAIRS)
    held = []

    def start():
        for tiles in phases(u_ref, seg, count):
            shifted = []
            for p in range(PAIRS + 1):
                back = pltpu.roll(tiles[p], LANES - 1, 1)
                on = pltpu.roll(tiles[p + 1], 1, 1)
                shifted.append(jnp.where(even, back, on))
            held.append(
                [
                    jnp.concatenate(part, axis=0).astype(jnp.bfloat16)
                    for part in (tiles[1 : PAIRS + 1], shifted[:PAIRS], shifted[1:])
                ]
            )

    def one(which, index):
        now, early, late = held[which]
        s = 2 * index - HALF
        if s > 0:
            z = jnp.where(wide >= LANES - s, early, now)
        elif s < 0:
            z = jnp.where(wide < -s, late, now)
        else:
            z = now
        z = pltpu.roll(z, lax.rem(off + (s + LANES), LANES), 1)
        for p in range(PAIRS):
            a_refs[which][index * count : (index + 1) * count, p * LANES : (p + 1) * LANES] = z[
                p * count : (p + 1) * count
            ]

    work = [start]
    for which, lag_count in enumerate((EVEN, EVEN, ODD)):
        work += [functools.partial(one, which, index) for index in range(lag_count)]
    return work


def power_kernel(begin, offsets_ref, x_ref, gain_ref):
    off = offsets_ref[begin + pl.program_id(0)]
    channels = x_ref.shape[0]
    early = lanes(ROWS) < off

    def square(at, m):
        value = x_ref[at : at + ROWS, m * LANES : (m + 1) * LANES].astype(jnp.float32)
        return value * value

    for row in range(0, channels, LANES):
        sums = []
        for at in range(row, min(row + LANES, channels), ROWS):
            total = jnp.where(early, square(at, TILES), square(at, 0))
            for m in range(1, TILES):
                total = total + square(at, m)
            sums.append(total)
        across = jnp.concatenate(sums, axis=0)
        power = jnp.sum(jnp.transpose(across), axis=0, keepdims=True) / L
        gain_ref[0, :, row : row + across.shape[0]] = lax.rsqrt(power + EPSILON)


def prepare(x_ref, base, off, row, w_refs, at):
    lane = lanes(ROWS)
    early = lane < off
    even = lax.rem(lane + off, 2) == 0
    first_ref, second_ref, both_ref = w_refs

    def tile(m):
        return x_ref[row : row + ROWS, base + m * LANES : base + (m + 1) * LANES]

    for p in range(PAIRS):
        a, b, c = tile(2 * p), tile(2 * p + 1), tile(2 * p + 2)
        low = jnp.where(early, b, a)
        high = jnp.where(early, c, b)
        first = jnp.where(even, low, pltpu.roll(high, 1, 1))
        second = jnp.where(even, pltpu.roll(low, LANES - 1, 1), high)
        span = slice(p * LANES, (p + 1) * LANES)
        first_ref[at : at + ROWS, span] = first
        second_ref[at : at + ROWS, span] = second
        both_ref[at : at + ROWS, span] = first + second


def dot(a, b):
    return lax.dot_general(a, b, (((1,), (1,)), ((), ())), preferred_element_type=jnp.float32)


def stack_kernel(src_count, blocks, begin, leads, *refs):
    refs = list(refs)

    def take(number):
        taken = refs[:number]
        del refs[:number]
        return taken

    units = sum(len(block) for block in blocks)
    offsets_ref, win_ref, gain_ref = take(3)
    if leads:
        (u_ref,) = take(1)
    else:
        shared = take(3)
    x_refs = take(units)
    keep_ref, send_ref = take(2)
    if leads:
        shared = take(3)
        a_slots = (take(3), take(3))
    c1, c2, c3 = take(3)
    w_slots = (take(3), take(3))
    (stage,) = take(1)
    if leads:
        (sems,) = take(1)

    n = pl.program_id(0)
    last = pl.num_programs(0) - 1
    unit, stride = x_refs[0].shape[0], x_refs[0].shape[1] // 2
    per_unit = pl.cdiv(unit, LANES)
    count = c1.shape[1] // EVEN
    offs = (offsets_ref[2 * n], offsets_ref[2 * n + 1])

    @pl.when(n == 0)
    def _():
        for c in (c1, c2, c3):
            c[...] = jnp.zeros_like(c)
        if leads:
            for piece in builders(u_ref, 0, offs[0], a_slots[0], count):
                piece()

    places = [(half, block) for half in (0, 1) for block in range(len(blocks))]

    def pieces(k):
        half, block = places[k]
        work = []
        for at, number in enumerate(blocks[block]):
            for row in range(0, unit, ROWS):
                work.append(
                    functools.partial(
                        prepare, x_refs[number], half * stride, offs[half], row,
                        w_slots[k % 2], at * unit + row,
                    )
                )
        return work

    def copies(half):
        return [
            pltpu.make_async_copy(a, out.at[2 * n + half], sems.at[i])
            for i, (a, out) in enumerate(zip(a_slots[half], shared))
        ]

    for piece in pieces(0):
        piece()
    built = []
    for k, (half, block) in enumerate(places):
        if leads and block == 0:
            for copy in copies(half):
                copy.start()
            later = 2 * n + 1 if half == 0 else lax.rem(2 * n + 2, 2 * last + 2)
            built = builders(u_ref, later, offsets_ref[later], a_slots[1 - half], count)
        slots_left = 3 * (len(blocks) - block)
        todo = pieces(k + 1) if k + 1 < len(places) else []
        first, second, both = w_slots[k % 2]
        width = unit * len(blocks[block])
        start = blocks[block][0] * unit
        gain = gain_ref[2 * n + half, :, begin + start : begin + start + width]
        operands = a_slots[half] if leads else [a.at[half] for a in shared]
        for i, (a, w, c) in enumerate(zip(operands, (both, second, first), (c1, c2, c3))):
            term = dot(a[...], w[:width, :]) * gain
            for at, number in enumerate(blocks[block]):
                for lane in range(0, unit, LANES):
                    size = min(LANES, unit - lane)
                    here = at * unit + lane
                    c[number * per_unit + lane // LANES, :, :size] += term[:, here : here + size]
            share = pl.cdiv(len(todo), 3 - i)
            built_share = pl.cdiv(len(built), slots_left - i)
            for piece in todo[:share] + built[:built_share]:
                piece()
            todo, built = todo[share:], built[built_share:]
        if leads and block == len(blocks) - 1:
            for copy in copies(half):
                copy.wait()

    @pl.when(n == last)
    def _():
        c2[...] += c1[...]
        c3[...] += c1[:, : ODD * count, :]
        for slot in range(4):
            step = win_ref[0] ^ slot
            out = send_ref if slot % 2 else keep_ref
            for group in range(units * per_unit):
                start = group // per_unit * unit + group % per_unit * LANES
                width = min(LANES, unit - group % per_unit * LANES)
                evens, odds = c2.at[group], c3.at[group]
                for i in range(src_count):
                    row = step * src_count + i
                    here = i * LAGS
                    stage[pl.ds(here, EVEN, stride=2), :] = evens[pl.ds(row, EVEN, stride=count), :]
                    stage[pl.ds(here + 1, ODD, stride=2), :] = odds[pl.ds(row, ODD, stride=count), :]
                out[slot // 2, :, start : start + width] = stage[:, :width]


def exchange(value, axis, size, offsets, works):
    me = lax.axis_index(axis)

    def swap(v, bit):
        return lax.ppermute(v, axis, [(d, d ^ bit) for d in range(size)])

    def scatter(v, bit):
        low = me & bit == 0
        half = v.shape[0] // 2
        one, two = v[:half], v[half:]
        return jnp.where(low, one, two) + swap(jnp.where(low, two, one), bit)

    def whole(v, bit):
        return v + swap(v, bit)

    def gather(v, bit):
        low = me & bit == 0
        other = swap(v, bit)
        return jnp.concatenate([jnp.where(low, v, other), jnp.where(low, other, v)], axis=0)

    bits = [1 << b for b in range(2, size.bit_length() - 1)]
    plans = [
        [(scatter, p), (scatter, q)] + [(whole, b) for b in bits] + [(gather, q), (gather, p)]
        for p, q in ((1, 2), (2, 1))
    ]
    half = value.shape[0] // 2
    values = [value[:half], value[half:]]
    results = []
    works = list(works)
    for index, steps in enumerate(zip(*plans)):
        values = [step(v, bit) for v, (step, bit) in zip(values, steps)]
        left = len(plans[0]) - index
        share = pl.cdiv(len(works), left)
        now = [work(offsets) for work in works[:share]]
        works = works[share:]
        if works:
            values, now, offsets = lax.optimization_barrier((values, now, offsets))
        results += now
    return jnp.concatenate(values, axis=0), results


def solution(mesh):
    chan = mesh.shape["chan"]
    win = mesh.shape["win"]

    def body(records, offsets, src_index, quality):
        channels, samples = records.shape
        seg_count = offsets.shape[0]
        stride = samples // seg_count
        step_count, src_count = src_index.shape
        count = step_count * src_count
        flat = src_index.reshape(-1)
        own = (lax.div(flat, channels) == lax.axis_index("chan")).astype(jnp.int32)[:, None]
        rows = jnp.take(records, lax.rem(flat, channels), axis=0, mode="clip")
        smem = pl.BlockSpec(memory_space=pltpu.SMEM)
        vmem = pl.BlockSpec(memory_space=pltpu.VMEM)
        sources = pl.pallas_call(
            source_kernel,
            out_shape=jax.ShapeDtypeStruct((seg_count, count, L), jnp.bfloat16),
            in_specs=[smem, vmem, vmem],
            out_specs=vmem,
            compiler_params=pltpu.CompilerParams(vmem_limit_bytes=32 * 2**20),
            name="sources",
        )(offsets, rows, own)

        def power(begin, number):
            return lambda starts: pl.pallas_call(
                functools.partial(power_kernel, begin),
                grid=(number,),
                out_shape=jax.ShapeDtypeStruct((number, 1, channels), jnp.float32),
                in_specs=[smem, pl.BlockSpec((channels, stride), lambda g: (0, begin + g))],
                out_specs=pl.BlockSpec((1, 1, channels), lambda g: (g, 0, 0)),
                compiler_params=pltpu.CompilerParams(vmem_limit_bytes=32 * 2**20),
                cost_estimate=pl.CostEstimate(
                    flops=2 * number * channels * stride,
                    bytes_accessed=2 * number * channels * stride,
                    transcendentals=0,
                ),
                name="power",
            )(starts, records)

        cuts = [0, 2, 3, 5, 6, seg_count]
        works = [power(a, b - a) for a, b in zip(cuts, cuts[1:])]
        sources, gains = exchange(sources, "chan", chan, offsets, works)
        gain = jnp.concatenate(gains, axis=0)

        w = lax.axis_index("win").astype(jnp.int32).reshape(1)
        bf16 = functools.partial(pltpu.VMEM, dtype=jnp.bfloat16)
        f32 = functools.partial(pltpu.VMEM, dtype=jnp.float32)
        depth = L // 2
        unit = UNIT if channels % UNIT == 0 else math.gcd(channels, ROWS)
        units = channels // unit
        lead = pl.cdiv(3 * units, 5)
        row_counts = (EVEN * count, EVEN * count, ODD * count)
        a_shapes = [jax.ShapeDtypeStruct((seg_count, r, depth), jnp.bfloat16) for r in row_counts]

        def stacks(blocks, begin, leads, operands):
            number = sum(len(block) for block in blocks)
            wide = number * unit
            half = jax.ShapeDtypeStruct((2, src_count * LAGS, wide), jnp.float32)
            sizes = [
                max([len(b) for b in (blocks + blocks)[parity::2]]) * unit for parity in (0, 1)
            ]

            def place(index):
                return pl.BlockSpec((unit, 2 * stride), lambda n: (begin // unit + index, n))

            any_space = pl.BlockSpec(memory_space=pl.ANY)
            given = (
                [vmem]
                if leads
                else [pl.BlockSpec((2, r, depth), lambda n: (n, 0, 0)) for r in row_counts]
            )
            return pl.pallas_call(
                functools.partial(stack_kernel, src_count, blocks, begin, leads),
                grid=(seg_count // 2,),
                out_shape=[half, half] + (a_shapes if leads else []),
                in_specs=[smem, smem, vmem] + given + [place(i) for i in range(number)],
                out_specs=[vmem, vmem] + ([any_space] * 3 if leads else []),
                scratch_shapes=([bf16((r, depth)) for r in row_counts] * 2 if leads else [])
                + [f32((number * pl.cdiv(unit, LANES), r, LANES)) for r in row_counts]
                + [bf16((size, depth)) for size in sizes for _ in range(3)]
                + [f32((src_count * LAGS, LANES))]
                + ([pltpu.SemaphoreType.DMA((3,))] if leads else []),
                compiler_params=pltpu.CompilerParams(vmem_limit_bytes=58 * 2**20),
                cost_estimate=pl.CostEstimate(
                    flops=2 * seg_count * sum(row_counts) * depth * wide,
                    bytes_accessed=2 * wide * samples,
                    transcendentals=0,
                ),
                name="stacks",
            )(offsets, w, gain, *operands, *([records] * number))

        def swap(v, bit):
            return lax.ppermute(v, "win", [(d, d ^ bit) for d in range(win)])

        def combine(keep, send):
            pair = keep + swap(send, 1)
            return pair[0] + swap(pair[1].astype(jnp.bfloat16), 2).astype(jnp.float32)

        rest = units - lead
        lead_blocks = [[0], list(range(1, lead))] if lead > 1 else [[0]]
        keep, send, *operands = stacks(lead_blocks, 0, True, [sources])
        totals = [combine(keep, send)]
        if rest:
            keep, send = stacks([list(range(rest))], lead * unit, False, operands)
            totals.append(combine(keep, send))
        total = jnp.concatenate(totals, axis=1)
        scale = 1.0 / math.sqrt(seg_count * win * L)
        return (total * scale * quality.astype(jnp.float32)[None, :])[None]

    return jax.shard_map(
        body,
        mesh=mesh,
        in_specs=(P("chan", "win"), P("win"), P(), P("chan")),
        out_specs=P("win", None, "chan"),
        check_vma=False,
    )
```

```python
import functools
import math

import jax
import jax.numpy as jnp
from jax import lax
from jax.experimental import pallas as pl
from jax.experimental.pallas import tpu as pltpu
from jax.sharding import PartitionSpec as P

L = 3072
LAGS = 49
HALF = (LAGS - 1) // 2
EVEN = HALF + 1
ODD = HALF
EPSILON = 1e-06
LANES = 128
TILES = L // LANES
PAIRS = TILES // 2
ROWS = 64
COLUMNS = 512


def lanes(rows, dtype=jnp.int32):
    return lax.broadcasted_iota(dtype, (rows, LANES), 1)


def source_kernel(offsets_ref, rows_ref, own_ref, out_ref):
    count = rows_ref.shape[0]
    seg_count = out_ref.shape[0]
    stride = rows_ref.shape[1] // seg_count
    lane = lanes(count)
    owned = own_ref[...] > 0

    def one(g, carry):
        off = offsets_ref[g]
        back = lax.rem(LANES - off, LANES)
        base = g * stride
        tiles = []
        for m in range(TILES + 1):
            start = pl.multiple_of(base + m * LANES, LANES)
            tiles.append(rows_ref[:, pl.ds(start, LANES)].astype(jnp.float32))
        cut = [jnp.where(lane < off, tiles[m + 1], tiles[m]) for m in range(TILES)]
        total = cut[0] * cut[0]
        for m in range(1, TILES):
            total = total + cut[m] * cut[m]
        power = jnp.sum(total, axis=1, keepdims=True) / L
        root = jnp.sqrt(power + EPSILON)
        for m in range(TILES):
            white = jnp.where(owned, pltpu.roll(cut[m], back, 1) / root, 0.0)
            out_ref[g, :, m * LANES : (m + 1) * LANES] = white.astype(jnp.bfloat16)
        return carry

    lax.fori_loop(0, seg_count, one, 0)


def phases(u_ref, seg, count):
    lane = lanes(count)
    even = lane % 2 == 0
    zero = jnp.zeros((count, LANES), jnp.float32)

    def tile(m):
        if m < 0 or m >= TILES:
            return zero
        return u_ref[seg, :, m * LANES : (m + 1) * LANES].astype(jnp.float32)

    plain, ahead, behind = [], [], []
    for p in range(-1, PAIRS + 1):
        low, high, before = tile(2 * p), tile(2 * p + 1), tile(2 * p - 1)
        low_on = pltpu.roll(low, 1, 1)
        high_on = pltpu.roll(high, 1, 1)
        before_on = pltpu.roll(before, 1, 1)
        plain.append(jnp.where(even, low, high_on))
        ahead.append(jnp.where(even, pltpu.roll(low, LANES - 1, 1) - low, high - high_on))
        late_low = jnp.where(lane == 0, before_on, low_on)
        late_high = jnp.where(lane == 0, low_on, high_on)
        behind.append(jnp.where(even, late_low - low, pltpu.roll(late_high, 1, 1) - high_on))
    return plain, ahead, behind


def builders(u_ref, seg, off, a_refs, count):
    lane = lanes(count)
    even = lane % 2 == 0
    wide = lanes(count * PAIRS)
    held = []

    def start():
        for tiles in phases(u_ref, seg, count):
            shifted = []
            for p in range(PAIRS + 1):
                back = pltpu.roll(tiles[p], LANES - 1, 1)
                on = pltpu.roll(tiles[p + 1], 1, 1)
                shifted.append(jnp.where(even, back, on))
            held.append(
                [
                    jnp.concatenate(part, axis=0).astype(jnp.bfloat16)
                    for part in (tiles[1 : PAIRS + 1], shifted[:PAIRS], shifted[1:])
                ]
            )

    def one(which, index):
        now, early, late = held[which]
        s = 2 * index - HALF
        if s > 0:
            z = jnp.where(wide >= LANES - s, early, now)
        elif s < 0:
            z = jnp.where(wide < -s, late, now)
        else:
            z = now
        z = pltpu.roll(z, lax.rem(off + (s + LANES), LANES), 1)
        a_refs[which][:, index * count : (index + 1) * count, :] = z.reshape(PAIRS, count, LANES)

    work = [start]
    for which, lag_count in enumerate((EVEN, EVEN, ODD)):
        work += [functools.partial(one, which, index) for index in range(lag_count)]
    return work


def power_kernel(begin, offsets_ref, *refs):
    x_refs, gain_ref = refs[:-1], refs[-1]
    off = offsets_ref[begin + pl.program_id(0)]
    channels = x_refs[0].shape[0]
    early = lanes(ROWS) < off

    def square(at, m):
        value = x_refs[m][at : at + ROWS, :].astype(jnp.float32)
        return value * value

    for row in range(0, channels, LANES):
        sums = []
        for at in range(row, min(row + LANES, channels), ROWS):
            total = jnp.where(early, square(at, TILES), square(at, 0))
            for m in range(1, TILES):
                total = total + square(at, m)
            sums.append(total)
        across = jnp.concatenate(sums, axis=0)
        power = jnp.sum(jnp.transpose(across), axis=0, keepdims=True) / L
        gain_ref[0, :, row : row + across.shape[0]] = lax.rsqrt(power + EPSILON)


def prepare(x_refs, off, row, w_refs, at):
    lane = lanes(ROWS)
    early = lane < off
    even = lax.rem(lane + off, 2) == 0
    first_ref, second_ref, both_ref = w_refs

    def tile(m):
        return x_refs[m][row : row + ROWS, :]

    for p in range(PAIRS):
        a, b, c = tile(2 * p), tile(2 * p + 1), tile(2 * p + 2)
        low = jnp.where(early, b, a)
        high = jnp.where(early, c, b)
        first = jnp.where(even, low, pltpu.roll(high, 1, 1))
        second = jnp.where(even, pltpu.roll(low, LANES - 1, 1), high)
        first_ref[p, at : at + ROWS, :] = first
        second_ref[p, at : at + ROWS, :] = second
        both_ref[p, at : at + ROWS, :] = first + second


def dot(a_ref, w_ref, width):
    a = jnp.concatenate([a_ref[p] for p in range(PAIRS)], axis=1)
    w = jnp.concatenate([w_ref[p, :width, :] for p in range(PAIRS)], axis=1)
    return lax.dot_general(a, w, (((1,), (1,)), ((), ())), preferred_element_type=jnp.float32)


def stack_kernel(src_count, blocks, scale, offsets_ref, win_ref, gain_ref, quality_ref, u_ref, *refs):
    refs = list(refs)

    def take(number):
        taken = refs[:number]
        del refs[:number]
        return taken

    x_refs = take(TILES + 1)
    outs = take(2)
    a_slots = (take(3), take(3))
    c1, c2, c3 = take(3)
    w_slots = (take(3), take(3))
    n = pl.program_id(0)
    last = pl.num_programs(0) - 1
    off = offsets_ref[n]
    count = u_ref.shape[1]

    @pl.when(n == 0)
    def _():
        for c in (c1, c2, c3):
            c[...] = jnp.zeros_like(c)
        for piece in builders(u_ref, 0, off, a_slots[0], count):
            piece()

    def pieces(k):
        start, width = blocks[k]
        return [
            functools.partial(prepare, x_refs, off, start + at, w_slots[k % 2], at)
            for at in range(0, width, ROWS)
        ]

    def segment(parity):
        for piece in pieces(0):
            piece()
        later = jnp.minimum(n + 1, last)
        built = builders(u_ref, later, offsets_ref[later], a_slots[1 - parity], count)
        for k, (start, width) in enumerate(blocks):
            todo = pieces(k + 1) if k + 1 < len(blocks) else []
            first, second, both = w_slots[k % 2]
            gain = gain_ref[n, :, start : start + width]
            for i, (a, w, c) in enumerate(
                zip(a_slots[parity], (both, second, first), (c1, c2, c3))
            ):
                term = dot(a, w, width) * gain
                for at in range(0, width, LANES):
                    size = min(LANES, width - at)
                    c[(start + at) // LANES, :, :size] += term[:, at : at + size]
                share = pl.cdiv(len(todo), 3 - i)
                built_share = pl.cdiv(len(built), 3 * (len(blocks) - k) - i)
                for piece in todo[:share] + built[:built_share]:
                    piece()
                todo, built = todo[share:], built[built_share:]

    for parity in (0, 1):
        pl.when(n % 2 == parity)(functools.partial(segment, parity))

    @pl.when(n == last)
    def _():
        groups = c1.shape[0]
        for group in range(groups):
            usable = quality_ref[group : group + 1, :] * scale
            c2[group] = (c1[group] + c2[group]) * usable
            c3[group] = (c1[group, : ODD * count, :] + c3[group]) * usable
        for slot in range(4):
            step = win_ref[0] ^ slot
            out = outs[slot % 2]
            base = slot // 2 * src_count * LAGS * groups
            for group in range(groups):
                evens, odds = c2.at[group], c3.at[group]
                for i in range(src_count):
                    row = step * src_count + i
                    here = base + i * LAGS * groups + group
                    out[pl.ds(here, EVEN, stride=2 * groups), :] = evens[
                        pl.ds(row, EVEN, stride=count), :
                    ]
                    out[pl.ds(here + groups, ODD, stride=2 * groups), :] = odds[
                        pl.ds(row, ODD, stride=count), :
                    ]


def exchange(value, axis, size, offsets, works):
    me = lax.axis_index(axis)

    def swap(v, bit):
        return lax.ppermute(v, axis, [(d, d ^ bit) for d in range(size)])

    def scatter(v, bit):
        low = me & bit == 0
        half = v.shape[0] // 2
        one, two = v[:half], v[half:]
        return jnp.where(low, one, two) + swap(jnp.where(low, two, one), bit)

    def whole(v, bit):
        return v + swap(v, bit)

    def gather(v, bit):
        low = me & bit == 0
        other = swap(v, bit)
        return jnp.concatenate([jnp.where(low, v, other), jnp.where(low, other, v)], axis=0)

    bits = [1 << b for b in range(2, size.bit_length() - 1)]
    plans = [
        [(scatter, p), (scatter, q)] + [(whole, b) for b in bits] + [(gather, q), (gather, p)]
        for p, q in ((1, 2), (2, 1))
    ]
    half = value.shape[0] // 2
    values = [value[:half], value[half:]]
    results = []
    works = list(works)
    for index, steps in enumerate(zip(*plans)):
        values = [step(v, bit) for v, (step, bit) in zip(values, steps)]
        left = len(plans[0]) - index
        share = pl.cdiv(len(works), left)
        now = [work(offsets) for work in works[:share]]
        works = works[share:]
        if works:
            values, now, offsets = lax.optimization_barrier((values, now, offsets))
        results += now
    return jnp.concatenate(values, axis=0), results


def solution(mesh):
    chan = mesh.shape["chan"]
    win = mesh.shape["win"]

    def body(records, offsets, src_index, quality):
        channels, samples = records.shape
        seg_count = offsets.shape[0]
        stride = samples // seg_count
        step_count, src_count = src_index.shape
        count = step_count * src_count
        flat = src_index.reshape(-1)
        own = (lax.div(flat, channels) == lax.axis_index("chan")).astype(jnp.int32)[:, None]
        rows = jnp.take(records, lax.rem(flat, channels), axis=0, mode="clip")
        smem = pl.BlockSpec(memory_space=pltpu.SMEM)
        vmem = pl.BlockSpec(memory_space=pltpu.VMEM)
        sources = pl.pallas_call(
            source_kernel,
            out_shape=jax.ShapeDtypeStruct((seg_count, count, L), jnp.bfloat16),
            in_specs=[smem, vmem, vmem],
            out_specs=vmem,
            compiler_params=pltpu.CompilerParams(vmem_limit_bytes=32 * 2**20),
            name="sources",
        )(offsets, rows, own)

        def tiles(begin):
            per = stride // LANES

            def place(m):
                return pl.BlockSpec((channels, LANES), lambda g: (0, (begin + g) * per + m))

            return [place(m) for m in range(TILES + 1)]

        def power(begin, number):
            return lambda starts: pl.pallas_call(
                functools.partial(power_kernel, begin),
                grid=(number,),
                out_shape=jax.ShapeDtypeStruct((number, 1, channels), jnp.float32),
                in_specs=[smem] + tiles(begin),
                out_specs=pl.BlockSpec((1, 1, channels), lambda g: (g, 0, 0)),
                compiler_params=pltpu.CompilerParams(vmem_limit_bytes=32 * 2**20),
                cost_estimate=pl.CostEstimate(
                    flops=2 * number * channels * stride,
                    bytes_accessed=2 * number * channels * stride,
                    transcendentals=0,
                ),
                name="power",
            )(starts, *([records] * (TILES + 1)))

        cuts = [0, 2, 3, 5, 6, seg_count]
        works = [power(a, b - a) for a, b in zip(cuts, cuts[1:])]
        sources, gains = exchange(sources, "chan", chan, offsets, works)
        gain = jnp.concatenate(gains, axis=0)

        w = lax.axis_index("win").astype(jnp.int32).reshape(1)
        bf16 = functools.partial(pltpu.VMEM, dtype=jnp.bfloat16)
        f32 = functools.partial(pltpu.VMEM, dtype=jnp.float32)
        groups = pl.cdiv(channels, LANES)
        row_counts = (EVEN * count, EVEN * count, ODD * count)
        head = channels % COLUMNS or COLUMNS
        blocks = [(0, head)] + [(at, COLUMNS) for at in range(head, channels, COLUMNS)]
        sizes = [max([width for _, width in blocks[parity::2]] + [ROWS]) for parity in (0, 1)]
        usable = jnp.pad(quality.astype(jnp.float32), (0, groups * LANES - channels))
        half = jax.ShapeDtypeStruct((2 * src_count * LAGS * groups, LANES), jnp.float32)
        scale = 1.0 / math.sqrt(seg_count * win * L)
        keep, send = pl.pallas_call(
            functools.partial(stack_kernel, src_count, blocks, scale),
            grid=(seg_count,),
            out_shape=(half, half),
            in_specs=[smem, smem, vmem, vmem, vmem] + tiles(0),
            out_specs=(vmem, vmem),
            scratch_shapes=[bf16((PAIRS, r, LANES)) for r in row_counts] * 2
            + [f32((groups, r, LANES)) for r in row_counts]
            + [bf16((PAIRS, size, LANES)) for size in sizes for _ in range(3)],
            compiler_params=pltpu.CompilerParams(vmem_limit_bytes=58 * 2**20),
            cost_estimate=pl.CostEstimate(
                flops=seg_count * sum(row_counts) * L * channels,
                bytes_accessed=2 * channels * samples,
                transcendentals=0,
            ),
            name="stacks",
        )(offsets, w, gain, usable.reshape(groups, LANES), sources, *([records] * (TILES + 1)))

        def swap(v, bit):
            return lax.ppermute(v, "win", [(d, d ^ bit) for d in range(win)])

        pair = keep + swap(send, 1)
        cut = pair.shape[0] // 2
        total = pair[:cut] + swap(pair[cut:].astype(jnp.bfloat16), 2).astype(jnp.float32)
        return total.reshape(1, src_count * LAGS, groups * LANES)[..., :channels]

    return jax.shard_map(
        body,
        mesh=mesh,
        in_specs=(P("chan", "win"), P("win"), P(), P("chan")),
        out_specs=P("win", None, "chan"),
        check_vma=False,
    )
```

```python
import functools
import math

import jax
import jax.numpy as jnp
from jax import lax
from jax.experimental import pallas as pl
from jax.experimental.pallas import tpu as pltpu
from jax.sharding import PartitionSpec as P

L = 3072
LAGS = 49
HALF = (LAGS - 1) // 2
EPSILON = 1e-06
LANES = 128
TILES = L // LANES
COLUMNS = 512


def lanes(rows, dtype=jnp.int32):
    return lax.broadcasted_iota(dtype, (rows, LANES), 1)


def source_kernel(offsets_ref, rows_ref, own_ref, out_ref):
    count = rows_ref.shape[0]
    seg_count = out_ref.shape[0]
    stride = rows_ref.shape[1] // seg_count
    lane = lanes(count)
    owned = own_ref[...] > 0

    def one(g, carry):
        off = offsets_ref[g]
        back = lax.rem(LANES - off, LANES)
        base = g * stride
        tiles = []
        for m in range(TILES + 1):
            start = pl.multiple_of(base + m * LANES, LANES)
            tiles.append(rows_ref[:, pl.ds(start, LANES)].astype(jnp.float32))
        cut = [jnp.where(lane < off, tiles[m + 1], tiles[m]) for m in range(TILES)]
        total = cut[0] * cut[0]
        for m in range(1, TILES):
            total = total + cut[m] * cut[m]
        power = jnp.sum(total, axis=1, keepdims=True) / L
        root = jnp.sqrt(power + EPSILON)
        for m in range(TILES):
            white = jnp.where(owned, pltpu.roll(cut[m], back, 1) / root, 0.0)
            out_ref[g, :, m * LANES : (m + 1) * LANES] = white.astype(jnp.bfloat16)
        return carry

    lax.fori_loop(0, seg_count, one, 0)


def builders(u_ref, seg, off, a_ref, count):
    lane = lanes(count)
    wide = lanes(count * (TILES + 1))
    zero = jnp.zeros((count, LANES), jnp.bfloat16)
    held = []

    def start():
        plain = [u_ref[seg, :, m * LANES : (m + 1) * LANES] for m in range(TILES)]
        turned = [pltpu.roll(tile, lax.rem(off, LANES), 1) for tile in plain]
        early = lane < off
        moved = [
            jnp.where(early, before, after)
            for before, after in zip([zero] + turned, turned + [zero])
        ]
        for part in (moved, [zero] + moved[:-1], moved[1:] + [zero]):
            held.append(jnp.concatenate(part, axis=0))

    def one(index):
        now, before, after = held
        s = index - HALF
        if s > 0:
            z = pltpu.roll(jnp.where(wide >= LANES - s, before, now), s, 1)
        elif s < 0:
            z = pltpu.roll(jnp.where(wide < -s, after, now), LANES + s, 1)
        else:
            z = now
        z = z.reshape(TILES + 1, count, LANES)
        rows = slice(index * count, (index + 1) * count)
        a_ref[0, rows, :] = jnp.where(lane < off, z[TILES], z[0])
        a_ref[1:, rows, :] = z[1:TILES]

    return [start] + [functools.partial(one, index) for index in range(LAGS)]


def weigh(x_ref, off, row, size, gain_ref):
    early = lanes(size) < off

    def square(m):
        value = x_ref[row : row + size, m * LANES : (m + 1) * LANES].astype(jnp.float32)
        return value * value

    total = jnp.where(early, square(TILES), square(0))
    for m in range(1, TILES):
        total = total + square(m)
    power = jnp.sum(jnp.transpose(total), axis=0, keepdims=True) / L
    gain_ref[:, row : row + size] = lax.rsqrt(power + EPSILON)


def dot(a_ref, x_ref, off, start, width):
    a = jnp.concatenate([a_ref[m] for m in range(TILES)], axis=1)
    rows = slice(start, start + width)
    first = jnp.where(lanes(width) < off, x_ref[rows, L : L + LANES], x_ref[rows, :LANES])
    x = jnp.concatenate([first, x_ref[rows, LANES:L]], axis=1)
    return lax.dot_general(a, x, (((1,), (1,)), ((), ())), preferred_element_type=jnp.float32)


def stack_kernel(
    src_count, blocks, scale, offsets_ref, win_ref, quality_ref, u_ref, x_ref,
    keep_ref, send_ref, a0, a1, total, gain_ref,
):
    outs = (keep_ref, send_ref)
    slots = (a0, a1)
    n = pl.program_id(0)
    last = pl.num_programs(0) - 1
    off = offsets_ref[n]
    count = u_ref.shape[1]
    groups = total.shape[0]

    @pl.when(n == 0)
    def _():
        total[...] = jnp.zeros_like(total)
        for piece in builders(u_ref, 0, off, a0, count):
            piece()

    def pieces(k):
        start, width = blocks[k]
        return [
            functools.partial(
                weigh, x_ref, off, start + at, min(LANES, width - at), gain_ref
            )
            for at in range(0, width, LANES)
        ]

    def segment(parity):
        later = jnp.minimum(n + 1, last)
        built = builders(u_ref, later, offsets_ref[later], slots[1 - parity], count)
        for piece in pieces(0):
            piece()
        for k, (start, width) in enumerate(blocks):
            term = dot(slots[parity], x_ref, off, start, width)
            share = pl.cdiv(len(built), len(blocks) - k)
            for piece in (pieces(k + 1) if k + 1 < len(blocks) else []) + built[:share]:
                piece()
            built = built[share:]
            term = term * gain_ref[:, start : start + width]
            for at in range(0, width, LANES):
                size = min(LANES, width - at)
                total[(start + at) // LANES, :, :size] += term[:, at : at + size]

    for parity in (0, 1):
        pl.when(n % 2 == parity)(functools.partial(segment, parity))

    @pl.when(n == last)
    def _():
        for group in range(groups):
            total[group] = total[group] * (quality_ref[group : group + 1, :] * scale)
        for slot in range(4):
            step = win_ref[0] ^ slot
            base = slot // 2 * src_count * LAGS * groups
            for group in range(groups):
                for i in range(src_count):
                    here = base + i * LAGS * groups + group
                    outs[slot % 2][pl.ds(here, LAGS, stride=groups), :] = total.at[group][
                        pl.ds(step * src_count + i, LAGS, stride=count), :
                    ]


def exchange(value, axis, size):
    me = lax.axis_index(axis)

    def swap(v, bit):
        return lax.ppermute(v, axis, [(d, d ^ bit) for d in range(size)])

    def scatter(v, bit):
        low = me & bit == 0
        half = v.shape[0] // 2
        one, two = v[:half], v[half:]
        return jnp.where(low, one, two) + swap(jnp.where(low, two, one), bit)

    def whole(v, bit):
        return v + swap(v, bit)

    def gather(v, bit):
        low = me & bit == 0
        other = swap(v, bit)
        return jnp.concatenate([jnp.where(low, v, other), jnp.where(low, other, v)], axis=0)

    bits = [1 << b for b in range(2, size.bit_length() - 1)]
    plans = [
        [(scatter, p), (scatter, q)] + [(whole, b) for b in bits] + [(gather, q), (gather, p)]
        for p, q in ((1, 2), (2, 1))
    ]
    half = value.shape[0] // 2
    values = [value[:half], value[half:]]
    for steps in zip(*plans):
        values = [step(v, bit) for v, (step, bit) in zip(values, steps)]
    return jnp.concatenate(values, axis=0)


def solution(mesh):
    chan = mesh.shape["chan"]
    win = mesh.shape["win"]

    def body(records, offsets, src_index, quality):
        channels, samples = records.shape
        seg_count = offsets.shape[0]
        stride = samples // seg_count
        step_count, src_count = src_index.shape
        count = step_count * src_count
        flat = src_index.reshape(-1)
        own = (lax.div(flat, channels) == lax.axis_index("chan")).astype(jnp.int32)[:, None]
        rows = jnp.take(records, lax.rem(flat, channels), axis=0, mode="clip")
        smem = pl.BlockSpec(memory_space=pltpu.SMEM)
        vmem = pl.BlockSpec(memory_space=pltpu.VMEM)
        sources = pl.pallas_call(
            source_kernel,
            out_shape=jax.ShapeDtypeStruct((seg_count, count, L), jnp.bfloat16),
            in_specs=[smem, vmem, vmem],
            out_specs=vmem,
            compiler_params=pltpu.CompilerParams(vmem_limit_bytes=32 * 2**20),
            name="sources",
        )(offsets, rows, own)

        sources = exchange(sources, "chan", chan)

        w = lax.axis_index("win").astype(jnp.int32).reshape(1)
        groups = pl.cdiv(channels, LANES)
        rows = LAGS * count
        head = channels % COLUMNS or COLUMNS
        blocks = [(0, head)] + [(at, COLUMNS) for at in range(head, channels, COLUMNS)]
        usable = jnp.pad(quality.astype(jnp.float32), (0, groups * LANES - channels))
        half = jax.ShapeDtypeStruct((2 * src_count * LAGS * groups, LANES), jnp.float32)
        scale = 1.0 / math.sqrt(seg_count * win * L)
        keep, send = pl.pallas_call(
            functools.partial(stack_kernel, src_count, blocks, scale),
            grid=(seg_count,),
            out_shape=(half, half),
            in_specs=[
                smem,
                smem,
                vmem,
                vmem,
                pl.BlockSpec((channels, stride), lambda g: (0, g)),
            ],
            out_specs=(vmem, vmem),
            scratch_shapes=[pltpu.VMEM((TILES, rows, LANES), jnp.bfloat16)] * 2
            + [
                pltpu.VMEM((groups, rows, LANES), jnp.float32),
                pltpu.VMEM((1, groups * LANES), jnp.float32),
            ],
            compiler_params=pltpu.CompilerParams(vmem_limit_bytes=52 * 2**20),
            cost_estimate=pl.CostEstimate(
                flops=2 * seg_count * rows * L * channels,
                bytes_accessed=2 * channels * samples,
                transcendentals=0,
            ),
            name="stacks",
        )(offsets, w, usable.reshape(groups, LANES), sources, records)

        def swap(v, bit):
            return lax.ppermute(v, "win", [(d, d ^ bit) for d in range(win)])

        pair = keep + swap(send.astype(jnp.bfloat16), 1).astype(jnp.float32)
        cut = pair.shape[0] // 2
        total = pair[:cut] + swap(pair[cut:].astype(jnp.bfloat16), 2).astype(jnp.float32)
        return total.reshape(1, src_count * LAGS, groups * LANES)[..., :channels]

    return jax.shard_map(
        body,
        mesh=mesh,
        in_specs=(P("chan", "win"), P("win"), P(), P("chan")),
        out_specs=P("win", None, "chan"),
        check_vma=False,
    )
```

```python
import functools
import math

import jax
import jax.numpy as jnp
from jax import lax
from jax.experimental import pallas as pl
from jax.experimental.pallas import tpu as pltpu
from jax.sharding import PartitionSpec as P

L = 3072
LAGS = 49
HALF = (LAGS - 1) // 2
EPSILON = 1e-06
LANES = 128
TILES = L // LANES
COLUMNS = 512


def lanes(rows, dtype=jnp.int32):
    return lax.broadcasted_iota(dtype, (rows, LANES), 1)


def source_kernel(channels, offsets_ref, flat_ref, me_ref, rows_ref, out_ref):
    count = rows_ref.shape[0]
    seg_count = out_ref.shape[0]
    stride = rows_ref.shape[1] // seg_count
    lane = lanes(count)
    row = lax.broadcasted_iota(jnp.int32, (count, LANES), 0)
    holder = jnp.zeros((count, LANES), jnp.int32)
    for i in range(count):
        holder = jnp.where(row == i, lax.div(flat_ref[i], channels), holder)
    owned = holder == me_ref[0]

    def one(g, carry):
        off = offsets_ref[g]
        back = lax.rem(LANES - off, LANES)
        base = g * stride
        tiles = []
        for m in range(TILES + 1):
            start = pl.multiple_of(base + m * LANES, LANES)
            tiles.append(rows_ref[:, pl.ds(start, LANES)].astype(jnp.float32))
        cut = [jnp.where(lane < off, tiles[m + 1], tiles[m]) for m in range(TILES)]
        total = cut[0] * cut[0]
        for m in range(1, TILES):
            total = total + cut[m] * cut[m]
        power = jnp.sum(total, axis=1, keepdims=True) / L
        root = jnp.sqrt(power + EPSILON)
        for m in range(TILES):
            white = jnp.where(owned, pltpu.roll(cut[m], back, 1) / root, 0.0)
            out_ref[g, :, m * LANES : (m + 1) * LANES] = white.astype(jnp.bfloat16)
        return carry

    lax.fori_loop(0, seg_count, one, 0)


def builders(u_ref, seg, off, a_ref, count):
    lane = lanes(count)
    wide = lanes(count * (TILES + 1))
    zero = jnp.zeros((count, LANES), jnp.bfloat16)
    held = []

    def start():
        plain = [u_ref[seg, :, m * LANES : (m + 1) * LANES] for m in range(TILES)]
        turned = [pltpu.roll(tile, lax.rem(off, LANES), 1) for tile in plain]
        early = lane < off
        moved = [
            jnp.where(early, before, after)
            for before, after in zip([zero] + turned, turned + [zero])
        ]
        for part in (moved, [zero] + moved[:-1], moved[1:] + [zero]):
            held.append(jnp.concatenate(part, axis=0))

    def one(index):
        now, before, after = held
        s = index - HALF
        if s > 0:
            z = pltpu.roll(jnp.where(wide >= LANES - s, before, now), s, 1)
        elif s < 0:
            z = pltpu.roll(jnp.where(wide < -s, after, now), LANES + s, 1)
        else:
            z = now
        z = z.reshape(TILES + 1, count, LANES)
        rows = slice(index * count, (index + 1) * count)
        a_ref[0, rows, :] = jnp.where(lane < off, z[TILES], z[0])
        a_ref[1:, rows, :] = z[1:TILES]

    return [start] + [functools.partial(one, index) for index in range(LAGS)]


def weigh(x_ref, off, row, size, gain_ref):
    early = lanes(size) < off

    def square(m):
        value = x_ref[row : row + size, m * LANES : (m + 1) * LANES]
        return value * value

    squares = [jnp.where(early, square(TILES), square(0))]
    squares += [square(m) for m in range(1, TILES)]
    total = jnp.zeros((size, LANES), jnp.float32)
    for m in range(0, TILES, 4):
        four = (squares[m] + squares[m + 1]) + (squares[m + 2] + squares[m + 3])
        total = total + four.astype(jnp.float32)
    power = jnp.sum(jnp.transpose(total), axis=0, keepdims=True) / L
    gain_ref[:, row : row + size] = lax.rsqrt(power + EPSILON)


def dot(a_ref, x_ref, off, start, width, begin, end):
    a = jnp.concatenate([a_ref[m] for m in range(begin, end)], axis=1)
    rows = slice(start, start + width)
    x = x_ref[rows, max(begin, 1) * LANES : end * LANES]
    if begin == 0:
        first = jnp.where(lanes(width) < off, x_ref[rows, L : L + LANES], x_ref[rows, :LANES])
        x = jnp.concatenate([first, x], axis=1)
    return lax.dot_general(a, x, (((1,), (1,)), ((), ())), preferred_element_type=jnp.float32)


def stack_kernel(
    src_count, blocks, scale, offsets_ref, win_ref, quality_ref, u_ref, x_ref,
    keep_ref, send_ref, a0, a1, total, gain_ref, away_ref,
):
    outs = (keep_ref, away_ref)
    slots = (a0, a1)
    n = pl.program_id(0)
    last = pl.num_programs(0) - 1
    off = offsets_ref[n]
    count = u_ref.shape[1]
    groups = total.shape[0]

    @pl.when(n == 0)
    def _():
        total[...] = jnp.zeros_like(total)
        for piece in builders(u_ref, 0, off, a0, count):
            piece()

    def pieces(k):
        start, width = blocks[k]
        return [
            functools.partial(
                weigh, x_ref, off, start + at, min(LANES, width - at), gain_ref
            )
            for at in range(0, width, LANES)
        ]

    def segment(parity):
        later = jnp.minimum(n + 1, last)
        built = builders(u_ref, later, offsets_ref[later], slots[1 - parity], count)
        for piece in pieces(0):
            piece()
        for k, (start, width) in enumerate(blocks):
            cuts = (0, TILES) if width == COLUMNS else (0, TILES // 2, TILES)
            terms = [
                dot(slots[parity], x_ref, off, start, width, begin, end)
                for begin, end in zip(cuts, cuts[1:])
            ]
            share = pl.cdiv(len(built), len(blocks) - k)
            for piece in (pieces(k + 1) if k + 1 < len(blocks) else []) + built[:share]:
                piece()
            built = built[share:]
            term = sum(terms[1:], terms[0]) * gain_ref[:, start : start + width]
            for at in range(0, width, LANES):
                size = min(LANES, width - at)
                total[(start + at) // LANES, :, :size] += term[:, at : at + size]

    for parity in (0, 1):
        pl.when(n % 2 == parity)(functools.partial(segment, parity))

    @pl.when(n == last)
    def _():
        for group in range(groups):
            total[group] = total[group] * (quality_ref[group : group + 1, :] * scale)
        for slot in range(4):
            step = win_ref[0] ^ slot
            base = slot // 2 * src_count * LAGS * groups
            for group in range(groups):
                for i in range(src_count):
                    here = base + i * LAGS * groups + group
                    outs[slot % 2][pl.ds(here, LAGS, stride=groups), :] = total.at[group][
                        pl.ds(step * src_count + i, LAGS, stride=count), :
                    ]
        send_ref[...] = away_ref[...].astype(jnp.bfloat16)


def exchange(value, axis, size):
    me = lax.axis_index(axis)

    def swap(v, bit):
        return lax.ppermute(v, axis, [(d, d ^ bit) for d in range(size)])

    def scatter(v, bit):
        low = me & bit == 0
        half = v.shape[0] // 2
        one, two = v[:half], v[half:]
        return jnp.where(low, one, two) + swap(jnp.where(low, two, one), bit)

    def whole(v, bit):
        return v + swap(v, bit)

    def gather(v, bit):
        low = me & bit == 0
        other = swap(v, bit)
        return jnp.concatenate([jnp.where(low, v, other), jnp.where(low, other, v)], axis=0)

    bits = [1 << b for b in range(2, size.bit_length() - 1)]
    plans = [
        [(scatter, p), (scatter, q)] + [(whole, b) for b in bits] + [(gather, q), (gather, p)]
        for p, q in ((1, 2), (2, 1))
    ]
    half = value.shape[0] // 2
    values = [value[:half], value[half:]]
    for steps in zip(*plans):
        values = [step(v, bit) for v, (step, bit) in zip(values, steps)]
    return jnp.concatenate(values, axis=0)


def solution(mesh):
    chan = mesh.shape["chan"]
    win = mesh.shape["win"]

    def body(records, offsets, src_index, quality):
        channels, samples = records.shape
        seg_count = offsets.shape[0]
        stride = samples // seg_count
        step_count, src_count = src_index.shape
        count = step_count * src_count
        flat = src_index.reshape(-1)
        me = lax.axis_index("chan").astype(jnp.int32).reshape(1)
        rows = records.at[lax.rem(flat, channels)].get(mode="promise_in_bounds")
        smem = pl.BlockSpec(memory_space=pltpu.SMEM)
        vmem = pl.BlockSpec(memory_space=pltpu.VMEM)
        sources = pl.pallas_call(
            functools.partial(source_kernel, channels),
            out_shape=jax.ShapeDtypeStruct((seg_count, count, L), jnp.bfloat16),
            in_specs=[smem, smem, smem, vmem],
            out_specs=vmem,
            compiler_params=pltpu.CompilerParams(vmem_limit_bytes=32 * 2**20),
            name="sources",
        )(offsets, flat, me, rows)

        sources = exchange(sources, "chan", chan)

        w = lax.axis_index("win").astype(jnp.int32).reshape(1)
        groups = pl.cdiv(channels, LANES)
        rows = LAGS * count
        head = channels % COLUMNS or COLUMNS
        blocks = [(0, head)] + [(at, COLUMNS) for at in range(head, channels, COLUMNS)]
        usable = jnp.pad(quality.astype(jnp.float32), (0, groups * LANES - channels))
        half = jax.ShapeDtypeStruct((2 * src_count * LAGS * groups, LANES), jnp.float32)
        scale = 1.0 / math.sqrt(seg_count * win * L)
        keep, send = pl.pallas_call(
            functools.partial(stack_kernel, src_count, blocks, scale),
            grid=(seg_count,),
            out_shape=(half, jax.ShapeDtypeStruct(half.shape, jnp.bfloat16)),
            in_specs=[
                smem,
                smem,
                vmem,
                vmem,
                pl.BlockSpec((channels, stride), lambda g: (0, g)),
            ],
            out_specs=(vmem, vmem),
            scratch_shapes=[pltpu.VMEM((TILES, rows, LANES), jnp.bfloat16)] * 2
            + [
                pltpu.VMEM((groups, rows, LANES), jnp.float32),
                pltpu.VMEM((1, groups * LANES), jnp.float32),
                pltpu.VMEM(half.shape, jnp.float32),
            ],
            compiler_params=pltpu.CompilerParams(vmem_limit_bytes=52 * 2**20),
            cost_estimate=pl.CostEstimate(
                flops=2 * seg_count * rows * L * channels,
                bytes_accessed=2 * channels * samples,
                transcendentals=0,
            ),
            name="stacks",
        )(offsets, w, usable.reshape(groups, LANES), sources, records)

        def swap(v, bit):
            return lax.ppermute(v, "win", [(d, d ^ bit) for d in range(win)])

        pair = keep + swap(send, 1).astype(jnp.float32)
        cut = pair.shape[0] // 2
        total = pair[:cut] + swap(pair[cut:].astype(jnp.bfloat16), 2).astype(jnp.float32)
        return total.reshape(1, src_count * LAGS, groups * LANES)[..., :channels]

    return jax.shard_map(
        body,
        mesh=mesh,
        in_specs=(P("chan", "win"), P("win"), P(), P("chan")),
        out_specs=P("win", None, "chan"),
        check_vma=False,
    )
```

```python
import functools
import math

import jax
import jax.numpy as jnp
from jax import lax
from jax.experimental import pallas as pl
from jax.experimental.pallas import tpu as pltpu
from jax.sharding import PartitionSpec as P

L = 3072
LAGS = 49
HALF = (LAGS - 1) // 2
EPSILON = 1e-06
LANES = 128
TILES = L // LANES
COLUMNS = 512


def lanes(rows, dtype=jnp.int32):
    return lax.broadcasted_iota(dtype, (rows, LANES), 1)


def source_kernel(channels, offsets_ref, flat_ref, me_ref, rows_ref, out_ref):
    count = rows_ref.shape[0]
    seg_count = out_ref.shape[0]
    stride = rows_ref.shape[1] // seg_count
    lane = lanes(count)
    row = lax.broadcasted_iota(jnp.int32, (count, LANES), 0)
    holder = jnp.zeros((count, LANES), jnp.int32)
    for i in range(count):
        holder = jnp.where(row == i, lax.div(flat_ref[i], channels), holder)
    owned = holder == me_ref[0]

    def one(g, carry):
        off = offsets_ref[g]
        back = lax.rem(LANES - off, LANES)
        base = g * stride
        tiles = []
        for m in range(TILES + 1):
            start = pl.multiple_of(base + m * LANES, LANES)
            tiles.append(rows_ref[:, pl.ds(start, LANES)].astype(jnp.float32))
        cut = [jnp.where(lane < off, tiles[m + 1], tiles[m]) for m in range(TILES)]
        total = cut[0] * cut[0]
        for m in range(1, TILES):
            total = total + cut[m] * cut[m]
        power = jnp.sum(total, axis=1, keepdims=True) / L
        root = jnp.sqrt(power + EPSILON)
        for m in range(TILES):
            white = jnp.where(owned, pltpu.roll(cut[m], back, 1) / root, 0.0)
            out_ref[g, :, m * LANES : (m + 1) * LANES] = white.astype(jnp.bfloat16)
        return carry

    lax.fori_loop(0, seg_count, one, 0)


def builders(u_ref, seg, off, a_ref, count):
    lane = lanes(count)
    wide = lanes(count * (TILES + 1))
    zero = jnp.zeros((count, LANES), jnp.bfloat16)
    held = []

    def start():
        plain = [u_ref[seg, :, m * LANES : (m + 1) * LANES] for m in range(TILES)]
        turned = [pltpu.roll(tile, lax.rem(off, LANES), 1) for tile in plain]
        early = lane < off
        moved = [
            jnp.where(early, before, after)
            for before, after in zip([zero] + turned, turned + [zero])
        ]
        for part in (moved, [zero] + moved[:-1], moved[1:] + [zero]):
            held.append(jnp.concatenate(part, axis=0))

    def one(index):
        now, before, after = held
        s = index - HALF
        if s > 0:
            z = pltpu.roll(jnp.where(wide >= LANES - s, before, now), s, 1)
        elif s < 0:
            z = pltpu.roll(jnp.where(wide < -s, after, now), LANES + s, 1)
        else:
            z = now
        z = z.reshape(TILES + 1, count, LANES)
        rows = slice(index * count, (index + 1) * count)
        a_ref[0, rows, :] = jnp.where(lane < off, z[TILES], z[0])
        a_ref[1:, rows, :] = z[1:TILES]

    return [start] + [functools.partial(one, index) for index in range(LAGS)]


def weigh(x_ref, off, row, size, gain_ref):
    early = lanes(size) < off

    def square(m):
        value = x_ref[row : row + size, m * LANES : (m + 1) * LANES]
        return value * value

    squares = [jnp.where(early, square(TILES), square(0))]
    squares += [square(m) for m in range(1, TILES)]
    total = jnp.zeros((size, LANES), jnp.float32)
    for m in range(0, TILES, 4):
        four = (squares[m] + squares[m + 1]) + (squares[m + 2] + squares[m + 3])
        total = total + four.astype(jnp.float32)
    power = jnp.sum(jnp.transpose(total), axis=0, keepdims=True) / L
    gain_ref[:, row : row + size] = lax.rsqrt(power + EPSILON)


def dot(a_ref, x_ref, off, start, width, begin, end):
    a = jnp.concatenate([a_ref[m] for m in range(begin, end)], axis=1)
    rows = slice(start, start + width)
    x = x_ref[rows, max(begin, 1) * LANES : end * LANES]
    if begin == 0:
        first = jnp.where(lanes(width) < off, x_ref[rows, L : L + LANES], x_ref[rows, :LANES])
        x = jnp.concatenate([first, x], axis=1)
    return lax.dot_general(a, x, (((1,), (1,)), ((), ())), preferred_element_type=jnp.float32)


def stack_kernel(
    blocks, scale, offsets_ref, quality_ref, u_ref, records_ref,
    keep0, keep1, send0, send1, a0, a1, x0, x1, total, gain_ref, sems,
):
    slots = (a0, a1)
    x_slots = (x0, x1)
    stride = x0.shape[1]
    n = pl.program_id(0)
    last = pl.num_programs(0) - 1
    off = offsets_ref[n]
    count = u_ref.shape[1]
    groups = total.shape[0]

    def fetch(seg, slot):
        start = pl.multiple_of(seg * stride, LANES)
        return pltpu.make_async_copy(
            records_ref.at[:, pl.ds(start, stride)], x_slots[slot], sems.at[slot]
        )

    @pl.when(n == 0)
    def _():
        fetch(0, 0).start()
        total[...] = jnp.zeros_like(total)
        for piece in builders(u_ref, 0, off, a0, count):
            piece()

    def pieces(k, x_ref):
        start, width = blocks[k]
        return [
            functools.partial(
                weigh, x_ref, off, start + at, min(LANES, width - at), gain_ref
            )
            for at in range(0, width, LANES)
        ]

    def segment(parity):
        x_ref = x_slots[parity]
        fetch(n, parity).wait()

        @pl.when(n < last)
        def _():
            fetch(n + 1, 1 - parity).start()

        later = jnp.minimum(n + 1, last)
        built = builders(u_ref, later, offsets_ref[later], slots[1 - parity], count)
        for piece in pieces(0, x_ref):
            piece()
        for k, (start, width) in enumerate(blocks):
            cuts = (0, TILES) if width == COLUMNS else (0, TILES // 2, TILES)
            terms = [
                dot(slots[parity], x_ref, off, start, width, begin, end)
                for begin, end in zip(cuts, cuts[1:])
            ]
            share = pl.cdiv(len(built), len(blocks) - k)
            for piece in (pieces(k + 1, x_ref) if k + 1 < len(blocks) else []) + built[:share]:
                piece()
            built = built[share:]
            term = sum(terms[1:], terms[0]) * gain_ref[:, start : start + width]
            for at in range(0, width, LANES):
                size = min(LANES, width - at)
                total[(start + at) // LANES, :, :size] += term[:, at : at + size]

    for parity in (0, 1):
        pl.when(n % 2 == parity)(functools.partial(segment, parity))

    @pl.when(n == last)
    def _():
        low = lax.broadcasted_iota(jnp.int32, (LAGS, 8, LANES), 1) < 4
        for pair in range(groups // 2):
            parts = []
            for group in (2 * pair, 2 * pair + 1):
                sums = total[group] * (quality_ref[group : group + 1, :] * scale)
                parts.append(sums.reshape(LAGS, count, LANES))
            rows = slice(pair * LAGS * 8, (pair + 1) * LAGS * 8)
            for begin, outs in ((0, (keep0, keep1)), (8, (send0, send1))):
                a, b = (part[:, begin : begin + 8] for part in parts)
                near = jnp.where(low, a, pltpu.roll(b, 4, 1))
                far = jnp.where(low, pltpu.roll(a, 4, 1), b)
                for out, value in zip(outs, (near, far)):
                    out[rows, :] = value.reshape(LAGS * 8, LANES).astype(out.dtype)


def finish_kernel(src_count, keep_ref, core_ref, chip_ref, out_ref, total):
    total[...] = (
        keep_ref[...] + core_ref[...].astype(jnp.float32) + chip_ref[...].astype(jnp.float32)
    )
    groups = out_ref.shape[0] // (src_count * LAGS)
    for group in range(groups):
        for i in range(src_count):
            row = group // 2 * LAGS * 8 + group % 2 * 4 + i
            out_ref[pl.ds(i * LAGS * groups + group, LAGS, stride=groups), :] = total[
                pl.ds(row, LAGS, stride=8), :
            ]


def exchange(value, axis, size):
    me = lax.axis_index(axis)

    def swap(v, bit):
        return lax.ppermute(v, axis, [(d, d ^ bit) for d in range(size)])

    def scatter(v, bit):
        low = me & bit == 0
        half = v.shape[0] // 2
        one, two = v[:half], v[half:]
        return jnp.where(low, one, two) + swap(jnp.where(low, two, one), bit)

    def whole(v, bit):
        return v + swap(v, bit)

    def gather(v, bit):
        low = me & bit == 0
        other = swap(v, bit)
        return jnp.concatenate([jnp.where(low, v, other), jnp.where(low, other, v)], axis=0)

    bits = [1 << b for b in range(2, size.bit_length() - 1)]
    plans = [
        [(scatter, p), (scatter, q)] + [(whole, b) for b in bits] + [(gather, q), (gather, p)]
        for p, q in ((1, 2), (2, 1))
    ]
    half = value.shape[0] // 2
    values = [value[:half], value[half:]]
    for steps in zip(*plans):
        values = [step(v, bit) for v, (step, bit) in zip(values, steps)]
    return jnp.concatenate(values, axis=0)


def solution(mesh):
    chan = mesh.shape["chan"]
    win = mesh.shape["win"]

    def body(records, offsets, src_index, quality):
        channels, samples = records.shape
        seg_count = offsets.shape[0]
        stride = samples // seg_count
        step_count, src_count = src_index.shape
        count = step_count * src_count
        w = lax.axis_index("win")
        steps = [src_index[k : k + 1] for k in range(step_count)]
        steps = [jnp.where(w & 1 == 0, steps[k], steps[k ^ 1]) for k in range(step_count)]
        steps = [jnp.where(w & 2 == 0, steps[k], steps[k ^ 2]) for k in range(step_count)]
        flat = jnp.concatenate([steps[k] for k in (0, 2, 1, 3)], axis=0).reshape(-1)
        me = lax.axis_index("chan").astype(jnp.int32).reshape(1)
        rows = records.at[lax.rem(flat, channels)].get(mode="promise_in_bounds")
        smem = pl.BlockSpec(memory_space=pltpu.SMEM)
        vmem = pl.BlockSpec(memory_space=pltpu.VMEM)
        sources = pl.pallas_call(
            functools.partial(source_kernel, channels),
            out_shape=jax.ShapeDtypeStruct((seg_count, count, L), jnp.bfloat16),
            in_specs=[smem, smem, smem, vmem],
            out_specs=vmem,
            compiler_params=pltpu.CompilerParams(vmem_limit_bytes=32 * 2**20),
            name="sources",
        )(offsets, flat, me, rows)

        sources = exchange(sources, "chan", chan)

        groups = pl.cdiv(channels, LANES)
        even = groups + groups % 2
        rows = LAGS * count
        head = channels % COLUMNS or COLUMNS
        blocks = [(0, head)] + [(at, COLUMNS) for at in range(head, channels, COLUMNS)]
        usable = jnp.pad(quality.astype(jnp.float32), (0, even * LANES - channels))
        shape = (even // 2 * LAGS * 8, LANES)
        kept = jax.ShapeDtypeStruct(shape, jnp.float32)
        sent = jax.ShapeDtypeStruct(shape, jnp.bfloat16)
        scale = 1.0 / math.sqrt(seg_count * win * L)
        keep0, keep1, send0, send1 = pl.pallas_call(
            functools.partial(stack_kernel, blocks, scale),
            grid=(seg_count,),
            out_shape=(kept, kept, sent, sent),
            in_specs=[smem, vmem, vmem, pl.BlockSpec(memory_space=pl.ANY)],
            out_specs=(vmem,) * 4,
            scratch_shapes=[pltpu.VMEM((TILES, rows, LANES), jnp.bfloat16)] * 2
            + [pltpu.VMEM((channels, stride), jnp.bfloat16)] * 2
            + [
                pltpu.VMEM((even, rows, LANES), jnp.float32),
                pltpu.VMEM((1, even * LANES), jnp.float32),
                pltpu.SemaphoreType.DMA((2,)),
            ],
            compiler_params=pltpu.CompilerParams(vmem_limit_bytes=52 * 2**20),
            cost_estimate=pl.CostEstimate(
                flops=2 * seg_count * rows * L * channels,
                bytes_accessed=2 * channels * samples,
                transcendentals=0,
            ),
            name="stacks",
        )(offsets, usable.reshape(even, LANES), sources, records)

        def swap(v, bit):
            return lax.ppermute(v, "win", [(d, d ^ bit) for d in range(win)])

        far = keep1 + swap(send1, 1).astype(jnp.float32)
        chip = swap(far.astype(jnp.bfloat16), 2)
        core = swap(send0, 1)
        total = pl.pallas_call(
            functools.partial(finish_kernel, src_count),
            out_shape=jax.ShapeDtypeStruct((src_count * LAGS * groups, LANES), jnp.float32),
            in_specs=[vmem] * 3,
            out_specs=vmem,
            scratch_shapes=[pltpu.VMEM(shape, jnp.float32)],
            compiler_params=pltpu.CompilerParams(vmem_limit_bytes=16 * 2**20),
            name="finish",
        )(keep0, core, chip)
        return total.reshape(1, src_count * LAGS, groups * LANES)[..., :channels]

    return jax.shard_map(
        body,
        mesh=mesh,
        in_specs=(P("chan", "win"), P("win"), P(), P("chan")),
        out_specs=P("win", None, "chan"),
        check_vma=False,
    )
```

```python
import functools
import math

import jax
import jax.numpy as jnp
from jax import lax
from jax.experimental import pallas as pl
from jax.experimental.pallas import tpu as pltpu
from jax.sharding import PartitionSpec as P

L = 3072
LAGS = 49
HALF = (LAGS - 1) // 2
EPSILON = 1e-06
LANES = 128
TILES = L // LANES
COLUMNS = 256


def lanes(rows, dtype=jnp.int32):
    return lax.broadcasted_iota(dtype, (rows, LANES), 1)


def source_kernel(channels, offsets_ref, flat_ref, me_ref, rows_ref, out_ref):
    count = rows_ref.shape[0]
    seg_count = out_ref.shape[0]
    stride = rows_ref.shape[1] // seg_count
    lane = lanes(count)
    row = lax.broadcasted_iota(jnp.int32, (count, LANES), 0)
    holder = jnp.zeros((count, LANES), jnp.int32)
    for i in range(count):
        holder = jnp.where(row == i, lax.div(flat_ref[i], channels), holder)
    owned = holder == me_ref[0]

    def one(g, carry):
        off = offsets_ref[g]
        back = lax.rem(LANES - off, LANES)
        base = g * stride
        tiles = []
        for m in range(TILES + 1):
            start = pl.multiple_of(base + m * LANES, LANES)
            tiles.append(rows_ref[:, pl.ds(start, LANES)].astype(jnp.float32))
        cut = [jnp.where(lane < off, tiles[m + 1], tiles[m]) for m in range(TILES)]
        total = cut[0] * cut[0]
        for m in range(1, TILES):
            total = total + cut[m] * cut[m]
        power = jnp.sum(total, axis=1, keepdims=True) / L
        root = jnp.sqrt(power + EPSILON)
        for m in range(TILES):
            white = jnp.where(owned, pltpu.roll(cut[m], back, 1) / root, 0.0)
            out_ref[g, :, m * LANES : (m + 1) * LANES] = white.astype(jnp.bfloat16)
        return carry

    lax.fori_loop(0, seg_count, one, 0)


def hold(u_ref, seg, off, held_ref):
    count = u_ref.shape[1]
    early = lanes(count) < off
    zero = jnp.zeros((count, LANES), jnp.bfloat16)
    turned = [
        pltpu.roll(u_ref[seg, :, m * LANES : (m + 1) * LANES], lax.rem(off, LANES), 1)
        for m in range(TILES)
    ]
    moved = [
        jnp.where(early, before, after)
        for before, after in zip([zero] + turned, turned + [zero])
    ]
    for which, part in enumerate((moved, [zero] + moved[:-1], moved[1:] + [zero])):
        held_ref[which] = jnp.concatenate(part, axis=0)


def build(held_ref, index, off, a_ref, count):
    wide = lanes(held_ref.shape[1])
    s = index - HALF
    z = jnp.where(wide >= LANES - s, held_ref[1], jnp.where(wide < -s, held_ref[2], held_ref[0]))
    z = pltpu.roll(z, lax.rem(s + LANES, LANES), 1).reshape(TILES + 1, count, LANES)
    rows = pl.ds(pl.multiple_of(index * count, count), count)
    a_ref[0, rows, :] = jnp.where(lanes(count) < off, z[TILES], z[0])
    a_ref[1:, rows, :] = z[1:TILES]


def weigh(x_ref, off, start, group, size, gain_ref):
    early = lanes(size) < off

    def square(m):
        value = x_ref[pl.ds(start, size), m * LANES : (m + 1) * LANES]
        return value * value

    squares = [jnp.where(early, square(TILES), square(0))]
    squares += [square(m) for m in range(1, TILES)]
    total = jnp.zeros((size, LANES), jnp.float32)
    for m in range(0, TILES, 4):
        four = (squares[m] + squares[m + 1]) + (squares[m + 2] + squares[m + 3])
        total = total + four.astype(jnp.float32)
    power = jnp.sum(jnp.transpose(total), axis=0, keepdims=True) / L
    gain_ref[group, :, :size] = lax.rsqrt(power + EPSILON)


def dot(a_ref, x_ref, off, start, width):
    a = jnp.concatenate([a_ref[m] for m in range(TILES)], axis=1)
    rows = pl.ds(start, width)
    first = jnp.where(lanes(width) < off, x_ref[rows, L : L + LANES], x_ref[rows, :LANES])
    x = jnp.concatenate([first, x_ref[rows, LANES:L]], axis=1)
    return lax.dot_general(a, x, (((1,), (1,)), ((), ())), preferred_element_type=jnp.float32)


def stack_kernel(
    width, scale, offsets_ref, quality_ref, u_ref, x_ref,
    keep0, keep1, send0, send1, a0, a1, held_ref, total, gain_ref,
):
    slots = (a0, a1)
    n = pl.program_id(0)
    last = pl.num_programs(0) - 1
    off = offsets_ref[n]
    count = u_ref.shape[1]
    groups = total.shape[0]
    blocks = x_ref.shape[0] // width
    per_block = pl.cdiv(width, LANES)
    share = pl.cdiv(LAGS, blocks)

    def weigh_block(k):
        for q in range(per_block):
            at = q * LANES
            start = pl.multiple_of(k * width + at, 16)
            weigh(x_ref, off, start, k * per_block + q, min(LANES, width - at), gain_ref)

    @pl.when(n == 0)
    def _():
        total[...] = jnp.zeros_like(total)
        hold(u_ref, 0, off, held_ref)

        def first(index, carry):
            build(held_ref, index, off, a0, count)
            return carry

        lax.fori_loop(0, LAGS, first, 0)

    later = jnp.minimum(n + 1, last)
    later_off = offsets_ref[later]
    hold(u_ref, later, later_off, held_ref)
    weigh_block(0)

    def segment(parity):
        def block(k, carry):
            term = dot(slots[parity], x_ref, off, pl.multiple_of(k * width, 16), width)
            if blocks > 1:
                weigh_block(jnp.minimum(k + 1, blocks - 1))
            for i in range(share):
                index = jnp.minimum(k * share + i, LAGS - 1)
                build(held_ref, index, later_off, slots[1 - parity], count)
            for q in range(per_block):
                at, size = q * LANES, min(LANES, width - q * LANES)
                group = k * per_block + q
                total[group, :, :size] += term[:, at : at + size] * gain_ref[group, :, :size]
            return carry

        lax.fori_loop(0, blocks, block, 0)

    for parity in (0, 1):
        pl.when(n % 2 == parity)(functools.partial(segment, parity))

    @pl.when(n == last)
    def _():
        low = lax.broadcasted_iota(jnp.int32, (LAGS, 8, LANES), 1) < 4
        for pair in range(groups // 2):
            parts = []
            for group in (2 * pair, 2 * pair + 1):
                sums = total[group] * (quality_ref[group : group + 1, :] * scale)
                parts.append(sums.reshape(LAGS, count, LANES))
            rows = slice(pair * LAGS * 8, (pair + 1) * LAGS * 8)
            for begin, outs in ((0, (keep0, keep1)), (8, (send0, send1))):
                a, b = (part[:, begin : begin + 8] for part in parts)
                near = jnp.where(low, a, pltpu.roll(b, 4, 1))
                far = jnp.where(low, pltpu.roll(a, 4, 1), b)
                for out, value in zip(outs, (near, far)):
                    out[rows, :] = value.reshape(LAGS * 8, LANES).astype(out.dtype)


def finish_kernel(src_count, keep_ref, core_ref, chip_ref, out_ref, total):
    total[...] = (
        keep_ref[...] + core_ref[...].astype(jnp.float32) + chip_ref[...].astype(jnp.float32)
    )
    groups = out_ref.shape[0] // (src_count * LAGS)
    for group in range(groups):
        for i in range(src_count):
            row = group // 2 * LAGS * 8 + group % 2 * 4 + i
            out_ref[pl.ds(i * LAGS * groups + group, LAGS, stride=groups), :] = total[
                pl.ds(row, LAGS, stride=8), :
            ]


def exchange(value, axis, size):
    me = lax.axis_index(axis)

    def swap(v, bit):
        return lax.ppermute(v, axis, [(d, d ^ bit) for d in range(size)])

    def scatter(v, bit):
        low = me & bit == 0
        half = v.shape[0] // 2
        one, two = v[:half], v[half:]
        return jnp.where(low, one, two) + swap(jnp.where(low, two, one), bit)

    def whole(v, bit):
        return v + swap(v, bit)

    def gather(v, bit):
        low = me & bit == 0
        other = swap(v, bit)
        return jnp.concatenate([jnp.where(low, v, other), jnp.where(low, other, v)], axis=0)

    bits = [1 << b for b in range(2, size.bit_length() - 1)]
    plans = [
        [(scatter, p), (scatter, q)] + [(whole, b) for b in bits] + [(gather, q), (gather, p)]
        for p, q in ((1, 2), (2, 1))
    ]
    half = value.shape[0] // 2
    values = [value[:half], value[half:]]
    for steps in zip(*plans):
        values = [step(v, bit) for v, (step, bit) in zip(values, steps)]
    return jnp.concatenate(values, axis=0)


def solution(mesh):
    chan = mesh.shape["chan"]
    win = mesh.shape["win"]

    def body(records, offsets, src_index, quality):
        channels, samples = records.shape
        seg_count = offsets.shape[0]
        stride = samples // seg_count
        step_count, src_count = src_index.shape
        count = step_count * src_count
        w = lax.axis_index("win")
        steps = [src_index[k : k + 1] for k in range(step_count)]
        steps = [jnp.where(w & 1 == 0, steps[k], steps[k ^ 1]) for k in range(step_count)]
        steps = [jnp.where(w & 2 == 0, steps[k], steps[k ^ 2]) for k in range(step_count)]
        flat = jnp.concatenate([steps[k] for k in (0, 2, 1, 3)], axis=0).reshape(-1)
        me = lax.axis_index("chan").astype(jnp.int32).reshape(1)
        rows = records.at[lax.rem(flat, channels)].get(mode="promise_in_bounds")
        smem = pl.BlockSpec(memory_space=pltpu.SMEM)
        vmem = pl.BlockSpec(memory_space=pltpu.VMEM)
        sources = pl.pallas_call(
            functools.partial(source_kernel, channels),
            out_shape=jax.ShapeDtypeStruct((seg_count, count, L), jnp.bfloat16),
            in_specs=[smem, smem, smem, vmem],
            out_specs=vmem,
            compiler_params=pltpu.CompilerParams(vmem_limit_bytes=32 * 2**20),
            name="sources",
        )(offsets, flat, me, rows)

        sources = exchange(sources, "chan", chan)

        groups = pl.cdiv(channels, LANES)
        even = groups + groups % 2
        rows = LAGS * count
        width = COLUMNS if channels % COLUMNS == 0 else channels
        usable = jnp.pad(quality.astype(jnp.float32), (0, even * LANES - channels))
        shape = (even // 2 * LAGS * 8, LANES)
        kept = jax.ShapeDtypeStruct(shape, jnp.float32)
        sent = jax.ShapeDtypeStruct(shape, jnp.bfloat16)
        scale = 1.0 / math.sqrt(seg_count * win * L)
        keep0, keep1, send0, send1 = pl.pallas_call(
            functools.partial(stack_kernel, width, scale),
            grid=(seg_count,),
            out_shape=(kept, kept, sent, sent),
            in_specs=[smem, vmem, vmem, pl.BlockSpec((channels, stride), lambda g: (0, g))],
            out_specs=(vmem,) * 4,
            scratch_shapes=[pltpu.VMEM((TILES, rows, LANES), jnp.bfloat16)] * 2
            + [
                pltpu.VMEM((3, (TILES + 1) * count, LANES), jnp.bfloat16),
                pltpu.VMEM((even, rows, LANES), jnp.float32),
                pltpu.VMEM((even, 1, LANES), jnp.float32),
            ],
            compiler_params=pltpu.CompilerParams(vmem_limit_bytes=52 * 2**20),
            cost_estimate=pl.CostEstimate(
                flops=2 * seg_count * rows * L * channels,
                bytes_accessed=2 * channels * samples,
                transcendentals=0,
            ),
            name="stacks",
        )(offsets, usable.reshape(even, LANES), sources, records)

        def swap(v, bit):
            return lax.ppermute(v, "win", [(d, d ^ bit) for d in range(win)])

        far = keep1 + swap(send1, 1).astype(jnp.float32)
        chip = swap(far.astype(jnp.bfloat16), 2)
        core = swap(send0, 1)
        total = pl.pallas_call(
            functools.partial(finish_kernel, src_count),
            out_shape=jax.ShapeDtypeStruct((src_count * LAGS * groups, LANES), jnp.float32),
            in_specs=[vmem] * 3,
            out_specs=vmem,
            scratch_shapes=[pltpu.VMEM(shape, jnp.float32)],
            compiler_params=pltpu.CompilerParams(vmem_limit_bytes=16 * 2**20),
            name="finish",
        )(keep0, core, chip)
        return total.reshape(1, src_count * LAGS, groups * LANES)[..., :channels]

    return jax.shard_map(
        body,
        mesh=mesh,
        in_specs=(P("chan", "win"), P("win"), P(), P("chan")),
        out_specs=P("win", None, "chan"),
        check_vma=False,
    )
```

```python
import functools
import math

import jax
import jax.numpy as jnp
from jax import lax
from jax.experimental import pallas as pl
from jax.experimental.pallas import tpu as pltpu
from jax.sharding import PartitionSpec as P

L = 3072
LAGS = 49
HALF = (LAGS - 1) // 2
EPSILON = 1e-06
LANES = 128
TILES = L // LANES
COLUMNS = 512


def lanes(rows, dtype=jnp.int32):
    return lax.broadcasted_iota(dtype, (rows, LANES), 1)


def source_kernel(channels, offsets_ref, flat_ref, me_ref, rows_ref, out_ref):
    count = rows_ref.shape[0]
    seg_count = out_ref.shape[0]
    stride = rows_ref.shape[1] // seg_count
    lane = lanes(count)
    row = lax.broadcasted_iota(jnp.int32, (count, LANES), 0)
    holder = jnp.zeros((count, LANES), jnp.int32)
    for i in range(count):
        holder = jnp.where(row == i, lax.div(flat_ref[i], channels), holder)
    owned = holder == me_ref[0]

    def one(g, carry):
        off = offsets_ref[g]
        back = lax.rem(LANES - off, LANES)
        base = g * stride
        tiles = []
        for m in range(TILES + 1):
            start = pl.multiple_of(base + m * LANES, LANES)
            tiles.append(rows_ref[:, pl.ds(start, LANES)].astype(jnp.float32))
        cut = [jnp.where(lane < off, tiles[m + 1], tiles[m]) for m in range(TILES)]
        total = cut[0] * cut[0]
        for m in range(1, TILES):
            total = total + cut[m] * cut[m]
        power = jnp.sum(total, axis=1, keepdims=True) / L
        root = jnp.sqrt(power + EPSILON)
        for m in range(TILES):
            white = jnp.where(owned, pltpu.roll(cut[m], back, 1) / root, 0.0)
            out_ref[g, :, m * LANES : (m + 1) * LANES] = white.astype(jnp.bfloat16)
        return carry

    lax.fori_loop(0, seg_count, one, 0)


def builders(u_ref, seg, off, a_ref, count):
    lane = lanes(count)
    wide = lanes(count * (TILES + 1))
    zero = jnp.zeros((count, LANES), jnp.bfloat16)
    held = []

    def start():
        plain = [u_ref[seg, :, m * LANES : (m + 1) * LANES] for m in range(TILES)]
        turned = [pltpu.roll(tile, lax.rem(off, LANES), 1) for tile in plain]
        early = lane < off
        moved = [
            jnp.where(early, before, after)
            for before, after in zip([zero] + turned, turned + [zero])
        ]
        for part in (moved, [zero] + moved[:-1], moved[1:] + [zero]):
            held.append(jnp.concatenate(part, axis=0))

    def one(index):
        now, before, after = held
        s = index - HALF
        if s > 0:
            z = pltpu.roll(jnp.where(wide >= LANES - s, before, now), s, 1)
        elif s < 0:
            z = pltpu.roll(jnp.where(wide < -s, after, now), LANES + s, 1)
        else:
            z = now
        z = z.reshape(TILES + 1, count, LANES)
        rows = slice(index * count, (index + 1) * count)
        a_ref[0, rows, :] = jnp.where(lane < off, z[TILES], z[0])
        a_ref[1:, rows, :] = z[1:TILES]

    return [start] + [functools.partial(one, index) for index in range(LAGS)]


def weigh(x_ref, off, row, size, gain_ref):
    early = lanes(size) < off

    def square(m):
        value = x_ref[row : row + size, m * LANES : (m + 1) * LANES]
        return value * value

    squares = [jnp.where(early, square(TILES), square(0))]
    squares += [square(m) for m in range(1, TILES)]
    total = jnp.zeros((size, LANES), jnp.float32)
    for m in range(0, TILES, 4):
        four = (squares[m] + squares[m + 1]) + (squares[m + 2] + squares[m + 3])
        total = total + four.astype(jnp.float32)
    power = jnp.sum(jnp.transpose(total), axis=0, keepdims=True) / L
    gain_ref[:, row : row + size] = lax.rsqrt(power + EPSILON)


def dot(a_ref, x_ref, off, start, width, begin, end):
    a = jnp.concatenate([a_ref[m] for m in range(begin, end)], axis=1)
    rows = slice(start, start + width)
    x = x_ref[rows, max(begin, 1) * LANES : end * LANES]
    if begin == 0:
        first = jnp.where(lanes(width) < off, x_ref[rows, L : L + LANES], x_ref[rows, :LANES])
        x = jnp.concatenate([first, x], axis=1)
    return lax.dot_general(a, x, (((1,), (1,)), ((), ())), preferred_element_type=jnp.float32)


def stack_kernel(
    blocks, scale, offsets_ref, quality_ref, u_ref, x_ref,
    keep0, keep1, send0, send1, a0, a1, total, gain_ref,
):
    slots = (a0, a1)
    n = pl.program_id(0)
    last = pl.num_programs(0) - 1
    off = offsets_ref[n]
    count = u_ref.shape[1]
    groups = total.shape[0]

    @pl.when(n == 0)
    def _():
        total[...] = jnp.zeros_like(total)
        for piece in builders(u_ref, 0, off, a0, count):
            piece()

    def pieces(k, x_ref):
        start, width = blocks[k]
        return [
            functools.partial(
                weigh, x_ref, off, start + at, min(LANES, width - at), gain_ref
            )
            for at in range(0, width, LANES)
        ]

    def segment(parity):
        later = jnp.minimum(n + 1, last)
        built = builders(u_ref, later, offsets_ref[later], slots[1 - parity], count)
        for piece in pieces(0, x_ref):
            piece()
        for k, (start, width) in enumerate(blocks):
            cuts = (0, TILES) if width == COLUMNS else (0, TILES // 2, TILES)
            terms = [
                dot(slots[parity], x_ref, off, start, width, begin, end)
                for begin, end in zip(cuts, cuts[1:])
            ]
            share = pl.cdiv(len(built), len(blocks) - k)
            for piece in (pieces(k + 1, x_ref) if k + 1 < len(blocks) else []) + built[:share]:
                piece()
            built = built[share:]
            term = sum(terms[1:], terms[0]) * gain_ref[:, start : start + width]
            for at in range(0, width, LANES):
                size = min(LANES, width - at)
                total[(start + at) // LANES, :, :size] += term[:, at : at + size]

    for parity in (0, 1):
        pl.when(n % 2 == parity)(functools.partial(segment, parity))

    @pl.when(n == last)
    def _():
        low = lax.broadcasted_iota(jnp.int32, (LAGS, 8, LANES), 1) < 4
        for pair in range(groups // 2):
            parts = []
            for group in (2 * pair, 2 * pair + 1):
                sums = total[group] * (quality_ref[group : group + 1, :] * scale)
                parts.append(sums.reshape(LAGS, count, LANES))
            rows = slice(pair * LAGS * 8, (pair + 1) * LAGS * 8)
            for begin, outs in ((0, (keep0, keep1)), (8, (send0, send1))):
                a, b = (part[:, begin : begin + 8] for part in parts)
                near = jnp.where(low, a, pltpu.roll(b, 4, 1))
                far = jnp.where(low, pltpu.roll(a, 4, 1), b)
                for out, value in zip(outs, (near, far)):
                    out[rows, :] = value.reshape(LAGS * 8, LANES).astype(out.dtype)


def finish_kernel(src_count, near_ref, chip_ref, out_ref, total):
    total[...] = near_ref[...] + chip_ref[...].astype(jnp.float32)
    groups = out_ref.shape[0] // (src_count * LAGS)
    for group in range(groups):
        for i in range(src_count):
            row = group // 2 * LAGS * 8 + group % 2 * 4 + i
            out_ref[pl.ds(i * LAGS * groups + group, LAGS, stride=groups), :] = total[
                pl.ds(row, LAGS, stride=8), :
            ]


def exchange(value, axis, size):
    me = lax.axis_index(axis)

    def swap(v, bit):
        return lax.ppermute(v, axis, [(d, d ^ bit) for d in range(size)])

    def scatter(v, bit):
        low = me & bit == 0
        half = v.shape[0] // 2
        one, two = v[:half], v[half:]
        return jnp.where(low, one, two) + swap(jnp.where(low, two, one), bit)

    def whole(v, bit):
        return v + swap(v, bit)

    def gather(v, bit):
        low = me & bit == 0
        other = swap(v, bit)
        return jnp.concatenate([jnp.where(low, v, other), jnp.where(low, other, v)], axis=0)

    bits = [1 << b for b in range(2, size.bit_length() - 1)]
    plans = [
        [(scatter, p), (scatter, q)] + [(whole, b) for b in bits] + [(gather, q), (gather, p)]
        for p, q in ((1, 2), (2, 1))
    ]
    half = value.shape[0] // 2
    values = [value[:half], value[half:]]
    for steps in zip(*plans):
        values = [step(v, bit) for v, (step, bit) in zip(values, steps)]
    return jnp.concatenate(values, axis=0)


def solution(mesh):
    chan = mesh.shape["chan"]
    win = mesh.shape["win"]

    def body(records, offsets, src_index, quality):
        channels, samples = records.shape
        seg_count = offsets.shape[0]
        stride = samples // seg_count
        step_count, src_count = src_index.shape
        count = step_count * src_count
        w = lax.axis_index("win")
        steps = [src_index[k : k + 1] for k in range(step_count)]
        steps = [jnp.where(w & 1 == 0, steps[k], steps[k ^ 1]) for k in range(step_count)]
        steps = [jnp.where(w & 2 == 0, steps[k], steps[k ^ 2]) for k in range(step_count)]
        flat = jnp.concatenate([steps[k] for k in (0, 2, 1, 3)], axis=0).reshape(-1)
        me = lax.axis_index("chan").astype(jnp.int32).reshape(1)
        rows = records.at[lax.rem(flat, channels)].get(mode="promise_in_bounds")
        smem = pl.BlockSpec(memory_space=pltpu.SMEM)
        vmem = pl.BlockSpec(memory_space=pltpu.VMEM)
        sources = pl.pallas_call(
            functools.partial(source_kernel, channels),
            out_shape=jax.ShapeDtypeStruct((seg_count, count, L), jnp.bfloat16),
            in_specs=[smem, smem, smem, vmem],
            out_specs=vmem,
            compiler_params=pltpu.CompilerParams(vmem_limit_bytes=32 * 2**20),
            name="sources",
        )(offsets, flat, me, rows)

        sources = exchange(sources, "chan", chan)

        groups = pl.cdiv(channels, LANES)
        even = groups + groups % 2
        rows = LAGS * count
        blocks = [(at, min(COLUMNS, channels - at)) for at in range(0, channels, COLUMNS)]
        usable = jnp.pad(quality.astype(jnp.float32), (0, even * LANES - channels))
        shape = (even // 2 * LAGS * 8, LANES)
        kept = jax.ShapeDtypeStruct(shape, jnp.float32)
        sent = jax.ShapeDtypeStruct(shape, jnp.bfloat16)
        scale = 1.0 / math.sqrt(seg_count * win * L)
        keep0, keep1, send0, send1 = pl.pallas_call(
            functools.partial(stack_kernel, blocks, scale),
            grid=(seg_count,),
            out_shape=(kept, kept, sent, sent),
            in_specs=[smem, vmem, vmem, pl.BlockSpec((channels, stride), lambda g: (0, g))],
            out_specs=(vmem,) * 4,
            scratch_shapes=[pltpu.VMEM((TILES, rows, LANES), jnp.bfloat16)] * 2
            + [
                pltpu.VMEM((even, rows, LANES), jnp.float32),
                pltpu.VMEM((1, even * LANES), jnp.float32),
            ],
            compiler_params=pltpu.CompilerParams(vmem_limit_bytes=52 * 2**20),
            cost_estimate=pl.CostEstimate(
                flops=2 * seg_count * rows * L * channels,
                bytes_accessed=2 * channels * samples,
                transcendentals=0,
            ),
            name="stacks",
        )(offsets, usable.reshape(even, LANES), sources, records)

        def swap(v, bit):
            return lax.ppermute(v, "win", [(d, d ^ bit) for d in range(win)])

        far = keep1 + swap(send1, 1).astype(jnp.float32)
        chip = swap(far.astype(jnp.bfloat16), 2)
        near = keep0 + swap(send0, 1).astype(jnp.float32)
        total = pl.pallas_call(
            functools.partial(finish_kernel, src_count),
            out_shape=jax.ShapeDtypeStruct((src_count * LAGS * groups, LANES), jnp.float32),
            in_specs=[vmem] * 2,
            out_specs=vmem,
            scratch_shapes=[pltpu.VMEM(shape, jnp.float32)],
            compiler_params=pltpu.CompilerParams(vmem_limit_bytes=16 * 2**20),
            name="finish",
        )(near, chip)
        return total.reshape(1, src_count * LAGS, groups * LANES)[..., :channels]

    return jax.shard_map(
        body,
        mesh=mesh,
        in_specs=(P("chan", "win"), P("win"), P(), P("chan")),
        out_specs=P("win", None, "chan"),
        check_vma=False,
    )
```

```python
import functools
import math

import jax
import jax.numpy as jnp
from jax import lax
from jax.experimental import pallas as pl
from jax.experimental.pallas import tpu as pltpu
from jax.sharding import PartitionSpec as P

L = 3072
LAGS = 49
HALF = (LAGS - 1) // 2
EPSILON = 1e-06
LANES = 128
TILES = L // LANES
COLUMNS = 1280


def lanes(rows, dtype=jnp.int32):
    return lax.broadcasted_iota(dtype, (rows, LANES), 1)


def source_kernel(channels, offsets_ref, flat_ref, me_ref, rows_ref, out_ref):
    count = rows_ref.shape[0]
    seg_count = out_ref.shape[0]
    stride = rows_ref.shape[1] // seg_count
    lane = lanes(count)
    row = lax.broadcasted_iota(jnp.int32, (count, LANES), 0)
    holder = jnp.zeros((count, LANES), jnp.int32)
    for i in range(count):
        holder = jnp.where(row == i, lax.div(flat_ref[i], channels), holder)
    owned = holder == me_ref[0]

    def one(g, carry):
        off = offsets_ref[g]
        back = lax.rem(LANES - off, LANES)
        base = g * stride
        tiles = []
        for m in range(TILES + 1):
            start = pl.multiple_of(base + m * LANES, LANES)
            tiles.append(rows_ref[:, pl.ds(start, LANES)].astype(jnp.float32))
        cut = [jnp.where(lane < off, tiles[m + 1], tiles[m]) for m in range(TILES)]
        total = cut[0] * cut[0]
        for m in range(1, TILES):
            total = total + cut[m] * cut[m]
        power = jnp.sum(total, axis=1, keepdims=True) / L
        root = jnp.sqrt(power + EPSILON)
        for m in range(TILES):
            white = jnp.where(owned, pltpu.roll(cut[m], back, 1) / root, 0.0)
            out_ref[g, :, m * LANES : (m + 1) * LANES] = white.astype(jnp.bfloat16)
        return carry

    lax.fori_loop(0, seg_count, one, 0)


def builders(u_ref, seg, off, a_ref, count):
    lane = lanes(count)
    wide = lanes(count * (TILES + 1))
    zero = jnp.zeros((count, LANES), jnp.bfloat16)
    held = []

    def start():
        plain = [u_ref[seg, :, m * LANES : (m + 1) * LANES] for m in range(TILES)]
        turned = [pltpu.roll(tile, lax.rem(off, LANES), 1) for tile in plain]
        early = lane < off
        moved = [
            jnp.where(early, before, after)
            for before, after in zip([zero] + turned, turned + [zero])
        ]
        for part in (moved, [zero] + moved[:-1], moved[1:] + [zero]):
            held.append(jnp.concatenate(part, axis=0))

    def one(index):
        now, before, after = held
        s = index - HALF
        if s > 0:
            z = pltpu.roll(jnp.where(wide >= LANES - s, before, now), s, 1)
        elif s < 0:
            z = pltpu.roll(jnp.where(wide < -s, after, now), LANES + s, 1)
        else:
            z = now
        z = z.reshape(TILES + 1, count, LANES)
        rows = slice(index * count, (index + 1) * count)
        a_ref[0, rows, :] = jnp.where(lane < off, z[TILES], z[0])
        a_ref[1:, rows, :] = z[1:TILES]

    return [start] + [functools.partial(one, index) for index in range(LAGS)]


def weigh(x_ref, off, row, size, gain_ref):
    early = lanes(size) < off

    def square(m):
        value = x_ref[row : row + size, m * LANES : (m + 1) * LANES]
        return value * value

    squares = [jnp.where(early, square(TILES), square(0))]
    squares += [square(m) for m in range(1, TILES)]
    total = jnp.zeros((size, LANES), jnp.float32)
    for m in range(0, TILES, 4):
        four = (squares[m] + squares[m + 1]) + (squares[m + 2] + squares[m + 3])
        total = total + four.astype(jnp.float32)
    power = jnp.sum(jnp.transpose(total), axis=0, keepdims=True) / L
    gain_ref[:, row : row + size] = lax.rsqrt(power + EPSILON)


def dot(a_ref, x_ref, off, start, width, begin, end):
    a = jnp.concatenate([a_ref[m] for m in range(begin, end)], axis=1)
    rows = slice(start, start + width)
    x = x_ref[rows, max(begin, 1) * LANES : end * LANES]
    if begin == 0:
        first = jnp.where(lanes(width) < off, x_ref[rows, L : L + LANES], x_ref[rows, :LANES])
        x = jnp.concatenate([first, x], axis=1)
    return lax.dot_general(a, x, (((1,), (1,)), ((), ())), preferred_element_type=jnp.float32)


def stack_kernel(
    blocks, scale, offsets_ref, quality_ref, u_ref, x_ref,
    keep0, keep1, send0, send1, a0, a1, total, gain_ref,
):
    slots = (a0, a1)
    n = pl.program_id(0)
    last = pl.num_programs(0) - 1
    off = offsets_ref[n]
    count = u_ref.shape[1]
    groups = total.shape[0]

    @pl.when(n == 0)
    def _():
        total[...] = jnp.zeros_like(total)
        for piece in builders(u_ref, 0, off, a0, count):
            piece()

    def pieces(k, x_ref):
        start, width = blocks[k]
        return [
            functools.partial(
                weigh, x_ref, off, start + at, min(LANES, width - at), gain_ref
            )
            for at in range(0, width, LANES)
        ]

    def segment(parity):
        later = jnp.minimum(n + 1, last)
        built = builders(u_ref, later, offsets_ref[later], slots[1 - parity], count)
        for piece in pieces(0, x_ref):
            piece()
        for k, (start, width) in enumerate(blocks):
            cuts = (0, TILES) if width == COLUMNS else (0, TILES // 2, TILES)
            terms = [
                dot(slots[parity], x_ref, off, start, width, begin, end)
                for begin, end in zip(cuts, cuts[1:])
            ]
            share = pl.cdiv(len(built), len(blocks) - k)
            for piece in (pieces(k + 1, x_ref) if k + 1 < len(blocks) else []) + built[:share]:
                piece()
            built = built[share:]
            term = sum(terms[1:], terms[0]) * gain_ref[:, start : start + width]
            for at in range(0, width, LANES):
                size = min(LANES, width - at)
                total[(start + at) // LANES, :, :size] += term[:, at : at + size]

    for parity in (0, 1):
        pl.when(n % 2 == parity)(functools.partial(segment, parity))

    @pl.when(n == last)
    def _():
        low = lax.broadcasted_iota(jnp.int32, (LAGS, 8, LANES), 1) < 4
        for pair in range(groups // 2):
            parts = []
            for group in (2 * pair, 2 * pair + 1):
                sums = total[group] * (quality_ref[group : group + 1, :] * scale)
                parts.append(sums.reshape(LAGS, count, LANES))
            rows = slice(pair * LAGS * 8, (pair + 1) * LAGS * 8)
            for begin, outs in ((0, (keep0, keep1)), (8, (send0, send1))):
                a, b = (part[:, begin : begin + 8] for part in parts)
                near = jnp.where(low, a, pltpu.roll(b, 4, 1))
                far = jnp.where(low, pltpu.roll(a, 4, 1), b)
                for out, value in zip(outs, (near, far)):
                    out[rows, :] = value.reshape(LAGS * 8, LANES).astype(out.dtype)


def finish_kernel(src_count, near_ref, chip_ref, out_ref, total):
    total[...] = near_ref[...] + chip_ref[...].astype(jnp.float32)
    groups = out_ref.shape[0] // (src_count * LAGS)
    for group in range(groups):
        for i in range(src_count):
            row = group // 2 * LAGS * 8 + group % 2 * 4 + i
            out_ref[pl.ds(i * LAGS * groups + group, LAGS, stride=groups), :] = total[
                pl.ds(row, LAGS, stride=8), :
            ]


def exchange(value, axis, size):
    me = lax.axis_index(axis)

    def swap(v, bit):
        return lax.ppermute(v, axis, [(d, d ^ bit) for d in range(size)])

    def scatter(v, bit):
        low = me & bit == 0
        half = v.shape[0] // 2
        one, two = v[:half], v[half:]
        return jnp.where(low, one, two) + swap(jnp.where(low, two, one), bit)

    def whole(v, bit):
        return v + swap(v, bit)

    def gather(v, bit):
        low = me & bit == 0
        other = swap(v, bit)
        return jnp.concatenate([jnp.where(low, v, other), jnp.where(low, other, v)], axis=0)

    bits = [1 << b for b in range(2, size.bit_length() - 1)]
    plans = [
        [(scatter, p), (scatter, q)] + [(whole, b) for b in bits] + [(gather, q), (gather, p)]
        for p, q in ((1, 2), (2, 1))
    ]
    half = value.shape[0] // 2
    values = [value[:half], value[half:]]
    for steps in zip(*plans):
        values = [step(v, bit) for v, (step, bit) in zip(values, steps)]
    return jnp.concatenate(values, axis=0)


def solution(mesh):
    chan = mesh.shape["chan"]
    win = mesh.shape["win"]

    def body(records, offsets, src_index, quality):
        channels, samples = records.shape
        seg_count = offsets.shape[0]
        stride = samples // seg_count
        step_count, src_count = src_index.shape
        count = step_count * src_count
        w = lax.axis_index("win")
        steps = [src_index[k : k + 1] for k in range(step_count)]
        steps = [jnp.where(w & 1 == 0, steps[k], steps[k ^ 1]) for k in range(step_count)]
        steps = [jnp.where(w & 2 == 0, steps[k], steps[k ^ 2]) for k in range(step_count)]
        flat = jnp.concatenate([steps[k] for k in (0, 2, 1, 3)], axis=0).reshape(-1)
        me = lax.axis_index("chan").astype(jnp.int32).reshape(1)
        rows = records.at[lax.rem(flat, channels)].get(mode="promise_in_bounds")
        smem = pl.BlockSpec(memory_space=pltpu.SMEM)
        vmem = pl.BlockSpec(memory_space=pltpu.VMEM)
        sources = pl.pallas_call(
            functools.partial(source_kernel, channels),
            out_shape=jax.ShapeDtypeStruct((seg_count, count, L), jnp.bfloat16),
            in_specs=[smem, smem, smem, vmem],
            out_specs=vmem,
            compiler_params=pltpu.CompilerParams(vmem_limit_bytes=32 * 2**20),
            name="sources",
        )(offsets, flat, me, rows)

        sources = exchange(sources, "chan", chan)

        groups = pl.cdiv(channels, LANES)
        even = groups + groups % 2
        rows = LAGS * count
        blocks = [(at, min(COLUMNS, channels - at)) for at in range(0, channels, COLUMNS)]
        usable = jnp.pad(quality.astype(jnp.float32), (0, even * LANES - channels))
        shape = (even // 2 * LAGS * 8, LANES)
        kept = jax.ShapeDtypeStruct(shape, jnp.float32)
        sent = jax.ShapeDtypeStruct(shape, jnp.bfloat16)
        scale = 1.0 / math.sqrt(seg_count * win * L)
        keep0, keep1, send0, send1 = pl.pallas_call(
            functools.partial(stack_kernel, blocks, scale),
            grid=(seg_count,),
            out_shape=(kept, kept, sent, sent),
            in_specs=[smem, vmem, vmem, pl.BlockSpec((channels, stride), lambda g: (0, g))],
            out_specs=(vmem,) * 4,
            scratch_shapes=[pltpu.VMEM((TILES, rows, LANES), jnp.bfloat16)] * 2
            + [
                pltpu.VMEM((even, rows, LANES), jnp.float32),
                pltpu.VMEM((1, even * LANES), jnp.float32),
            ],
            compiler_params=pltpu.CompilerParams(vmem_limit_bytes=52 * 2**20),
            cost_estimate=pl.CostEstimate(
                flops=2 * seg_count * rows * L * channels,
                bytes_accessed=2 * channels * samples,
                transcendentals=0,
            ),
            name="stacks",
        )(offsets, usable.reshape(even, LANES), sources, records)

        def swap(v, bit):
            return lax.ppermute(v, "win", [(d, d ^ bit) for d in range(win)])

        far = keep1 + swap(send1, 1).astype(jnp.float32)
        chip = swap(far.astype(jnp.bfloat16), 2)
        near = keep0 + swap(send0, 1).astype(jnp.float32)
        total = pl.pallas_call(
            functools.partial(finish_kernel, src_count),
            out_shape=jax.ShapeDtypeStruct((src_count * LAGS * groups, LANES), jnp.float32),
            in_specs=[vmem] * 2,
            out_specs=vmem,
            scratch_shapes=[pltpu.VMEM(shape, jnp.float32)],
            compiler_params=pltpu.CompilerParams(vmem_limit_bytes=16 * 2**20),
            name="finish",
        )(near, chip)
        return total.reshape(1, src_count * LAGS, groups * LANES)[..., :channels]

    return jax.shard_map(
        body,
        mesh=mesh,
        in_specs=(P("chan", "win"), P("win"), P(), P("chan")),
        out_specs=P("win", None, "chan"),
        check_vma=False,
    )
```

```python
import functools
import math

import jax
import jax.numpy as jnp
from jax import lax
from jax.experimental import pallas as pl
from jax.experimental.pallas import tpu as pltpu
from jax.sharding import PartitionSpec as P

L = 3072
LAGS = 49
HALF = (LAGS - 1) // 2
EPSILON = 1e-06
LANES = 128
TILES = L // LANES
ROWS = 64
COLUMNS = 512


def lanes(rows, dtype=jnp.int32):
    return lax.broadcasted_iota(dtype, (rows, LANES), 1)


def source_kernel(channels, offsets_ref, flat_ref, me_ref, rows_ref, out_ref):
    count = rows_ref.shape[0]
    seg_count = out_ref.shape[0]
    stride = rows_ref.shape[1] // seg_count
    lane = lanes(count)
    row = lax.broadcasted_iota(jnp.int32, (count, LANES), 0)
    holder = jnp.zeros((count, LANES), jnp.int32)
    for i in range(count):
        holder = jnp.where(row == i, lax.div(flat_ref[i], channels), holder)
    owned = holder == me_ref[0]

    def one(g, carry):
        off = offsets_ref[g]
        back = lax.rem(LANES - off, LANES)
        base = g * stride
        tiles = []
        for m in range(TILES + 1):
            start = pl.multiple_of(base + m * LANES, LANES)
            tiles.append(rows_ref[:, pl.ds(start, LANES)].astype(jnp.float32))
        cut = [jnp.where(lane < off, tiles[m + 1], tiles[m]) for m in range(TILES)]
        total = cut[0] * cut[0]
        for m in range(1, TILES):
            total = total + cut[m] * cut[m]
        power = jnp.sum(total, axis=1, keepdims=True) / L
        root = jnp.sqrt(power + EPSILON)
        for m in range(TILES):
            white = jnp.where(owned, pltpu.roll(cut[m], back, 1) / root, 0.0)
            out_ref[g, :, m * LANES : (m + 1) * LANES] = white.astype(jnp.bfloat16)
        return carry

    lax.fori_loop(0, seg_count, one, 0)


def builders(u_refs, seg, off, a_ref, count):
    lane = lanes(count)
    wide = lanes(count * (TILES + 1))
    zero = jnp.zeros((count, LANES), jnp.bfloat16)
    held = []

    def start():
        half = u_refs[0].shape[0]
        pick = lane < jnp.where(seg < half, LANES, 0)
        low, high = jnp.minimum(seg, half - 1), jnp.maximum(seg - half, 0)
        plain = []
        for m in range(TILES):
            span = slice(m * LANES, (m + 1) * LANES)
            plain.append(jnp.where(pick, u_refs[0][low, :, span], u_refs[1][high, :, span]))
        turned = [pltpu.roll(tile, lax.rem(off, LANES), 1) for tile in plain]
        early = lane < off
        moved = [
            jnp.where(early, before, after)
            for before, after in zip([zero] + turned, turned + [zero])
        ]
        for part in (moved, [zero] + moved[:-1], moved[1:] + [zero]):
            held.append(jnp.concatenate(part, axis=0))

    def one(index):
        now, before, after = held
        s = index - HALF
        if s > 0:
            z = pltpu.roll(jnp.where(wide >= LANES - s, before, now), s, 1)
        elif s < 0:
            z = pltpu.roll(jnp.where(wide < -s, after, now), LANES + s, 1)
        else:
            z = now
        z = z.reshape(TILES + 1, count, LANES)
        rows = slice(index * count, (index + 1) * count)
        a_ref[0, rows, :] = jnp.where(lane < off, z[TILES], z[0])
        a_ref[1:, rows, :] = z[1:TILES]

    return [start] + [functools.partial(one, index) for index in range(LAGS)]


def weigh(x_ref, off, row, size, gain_ref):
    parts = []
    for at in range(row, row + size, ROWS):
        early = lanes(ROWS) < off

        def square(m):
            value = x_ref[at : at + ROWS, m * LANES : (m + 1) * LANES]
            return value * value

        total = jnp.zeros((ROWS, LANES), jnp.float32)
        for m in range(0, TILES, 4):
            one = square(m) if m else jnp.where(early, square(TILES), square(0))
            four = (one + square(m + 1)) + (square(m + 2) + square(m + 3))
            total = total + four.astype(jnp.float32)
        parts.append(total)
    across = jnp.concatenate(parts, axis=0)
    power = jnp.sum(jnp.transpose(across), axis=0, keepdims=True) / L
    gain_ref[:, row : row + size] = lax.rsqrt(power + EPSILON)


def dot(a_ref, x_ref, off, start, width, begin, end):
    a = jnp.concatenate([a_ref[m] for m in range(begin, end)], axis=1)
    rows = slice(start, start + width)
    x = x_ref[rows, max(begin, 1) * LANES : end * LANES]
    if begin == 0:
        first = jnp.where(lanes(width) < off, x_ref[rows, L : L + LANES], x_ref[rows, :LANES])
        x = jnp.concatenate([first, x], axis=1)
    return lax.dot_general(a, x, (((1,), (1,)), ((), ())), preferred_element_type=jnp.float32)


def stack_kernel(
    blocks, scale, offsets_ref, quality_ref, u0, u1, x_ref,
    keep0, keep1, send0, send1, a0, a1, total, gain_ref,
):
    slots = (a0, a1)
    u_refs = (u0, u1)
    n = pl.program_id(0)
    last = pl.num_programs(0) - 1
    off = offsets_ref[n]
    count = u0.shape[1]
    groups = total.shape[0]

    @pl.when(n == 0)
    def _():
        total[...] = jnp.zeros_like(total)
        for piece in builders(u_refs, 0, off, a0, count):
            piece()

    def pieces(k, x_ref):
        start, width = blocks[k]
        return [
            functools.partial(
                weigh, x_ref, off, start + at, min(LANES, width - at), gain_ref
            )
            for at in range(0, width, LANES)
        ]

    def segment(parity):
        later = jnp.minimum(n + 1, last)
        built = builders(u_refs, later, offsets_ref[later], slots[1 - parity], count)
        for piece in pieces(0, x_ref):
            piece()
        for k, (start, width) in enumerate(blocks):
            cuts = (0, TILES) if width == COLUMNS else (0, TILES // 2, TILES)
            terms = [
                dot(slots[parity], x_ref, off, start, width, begin, end)
                for begin, end in zip(cuts, cuts[1:])
            ]
            share = pl.cdiv(len(built), len(blocks) - k)
            for piece in (pieces(k + 1, x_ref) if k + 1 < len(blocks) else []) + built[:share]:
                piece()
            built = built[share:]
            term = sum(terms[1:], terms[0]) * gain_ref[:, start : start + width]
            for at in range(0, width, LANES):
                size = min(LANES, width - at)
                total[(start + at) // LANES, :, :size] += term[:, at : at + size]

    for parity in (0, 1):
        pl.when(n % 2 == parity)(functools.partial(segment, parity))

    @pl.when(n == last)
    def _():
        low = lax.broadcasted_iota(jnp.int32, (LAGS, 8, LANES), 1) < 4
        for pair in range(groups // 2):
            parts = []
            for group in (2 * pair, 2 * pair + 1):
                sums = total[group] * (quality_ref[group : group + 1, :] * scale)
                parts.append(sums.reshape(LAGS, count, LANES))
            rows = slice(pair * LAGS * 8, (pair + 1) * LAGS * 8)
            for begin, outs in ((0, (keep0, keep1)), (8, (send0, send1))):
                a, b = (part[:, begin : begin + 8] for part in parts)
                near = jnp.where(low, a, pltpu.roll(b, 4, 1))
                far = jnp.where(low, pltpu.roll(a, 4, 1), b)
                for out, value in zip(outs, (near, far)):
                    out[rows, :] = value.reshape(LAGS * 8, LANES).astype(out.dtype)


def finish_kernel(src_count, near_ref, chip_ref, out_ref, total):
    total[...] = near_ref[...] + chip_ref[...].astype(jnp.float32)
    groups = out_ref.shape[0] // (src_count * LAGS)
    for group in range(groups):
        for i in range(src_count):
            row = group // 2 * LAGS * 8 + group % 2 * 4 + i
            out_ref[pl.ds(i * LAGS * groups + group, LAGS, stride=groups), :] = total[
                pl.ds(row, LAGS, stride=8), :
            ]


def exchange(value, axis, size):
    me = lax.axis_index(axis)

    def swap(v, bit):
        return lax.ppermute(v, axis, [(d, d ^ bit) for d in range(size)])

    def scatter(v, bit):
        low = me & bit == 0
        half = v.shape[0] // 2
        one, two = v[:half], v[half:]
        return jnp.where(low, one, two) + swap(jnp.where(low, two, one), bit)

    def whole(v, bit):
        return v + swap(v, bit)

    def gather(v, bit):
        low = me & bit == 0
        other = swap(v, bit)
        return jnp.concatenate([jnp.where(low, v, other), jnp.where(low, other, v)], axis=0)

    bits = [1 << b for b in range(2, size.bit_length() - 1)]
    plans = [
        [(scatter, p), (scatter, q)] + [(whole, b) for b in bits] + [(gather, q), (gather, p)]
        for p, q in ((1, 2), (2, 1))
    ]
    half = value.shape[0] // 2
    values = [value[:half], value[half:]]
    for steps in zip(*plans):
        values = [step(v, bit) for v, (step, bit) in zip(values, steps)]
    return values


def solution(mesh):
    chan = mesh.shape["chan"]
    win = mesh.shape["win"]

    def body(records, offsets, src_index, quality):
        channels, samples = records.shape
        seg_count = offsets.shape[0]
        stride = samples // seg_count
        step_count, src_count = src_index.shape
        count = step_count * src_count
        w = lax.axis_index("win")
        steps = [src_index[k : k + 1] for k in range(step_count)]
        steps = [jnp.where(w & 1 == 0, steps[k], steps[k ^ 1]) for k in range(step_count)]
        steps = [jnp.where(w & 2 == 0, steps[k], steps[k ^ 2]) for k in range(step_count)]
        flat = jnp.concatenate([steps[k] for k in (0, 2, 1, 3)], axis=0).reshape(-1)
        me = lax.axis_index("chan").astype(jnp.int32).reshape(1)
        rows = records.at[lax.rem(flat, channels)].get(mode="promise_in_bounds")
        smem = pl.BlockSpec(memory_space=pltpu.SMEM)
        vmem = pl.BlockSpec(memory_space=pltpu.VMEM)
        sources = pl.pallas_call(
            functools.partial(source_kernel, channels),
            out_shape=jax.ShapeDtypeStruct((seg_count, count, L), jnp.bfloat16),
            in_specs=[smem, smem, smem, vmem],
            out_specs=vmem,
            compiler_params=pltpu.CompilerParams(vmem_limit_bytes=32 * 2**20),
            name="sources",
        )(offsets, flat, me, rows)

        sources = exchange(sources, "chan", chan)

        groups = pl.cdiv(channels, LANES)
        even = groups + groups % 2
        rows = LAGS * count
        blocks = [(at, min(COLUMNS, channels - at)) for at in range(0, channels, COLUMNS)]
        usable = jnp.pad(quality.astype(jnp.float32), (0, even * LANES - channels))
        shape = (even // 2 * LAGS * 8, LANES)
        kept = jax.ShapeDtypeStruct(shape, jnp.float32)
        sent = jax.ShapeDtypeStruct(shape, jnp.bfloat16)
        scale = 1.0 / math.sqrt(seg_count * win * L)
        keep0, keep1, send0, send1 = pl.pallas_call(
            functools.partial(stack_kernel, blocks, scale),
            grid=(seg_count,),
            out_shape=(kept, kept, sent, sent),
            in_specs=[smem, vmem, vmem, vmem, pl.BlockSpec((channels, stride), lambda g: (0, g))],
            out_specs=(vmem,) * 4,
            scratch_shapes=[pltpu.VMEM((TILES, rows, LANES), jnp.bfloat16)] * 2
            + [
                pltpu.VMEM((even, rows, LANES), jnp.float32),
                pltpu.VMEM((1, even * LANES), jnp.float32),
            ],
            compiler_params=pltpu.CompilerParams(vmem_limit_bytes=52 * 2**20),
            cost_estimate=pl.CostEstimate(
                flops=2 * seg_count * rows * L * channels,
                bytes_accessed=2 * channels * samples,
                transcendentals=0,
            ),
            name="stacks",
        )(offsets, usable.reshape(even, LANES), *sources, records)

        def swap(v, bit):
            return lax.ppermute(v, "win", [(d, d ^ bit) for d in range(win)])

        far = keep1 + swap(send1, 1).astype(jnp.float32)
        chip = swap(far.astype(jnp.bfloat16), 2)
        near = keep0 + swap(send0, 1).astype(jnp.float32)
        total = pl.pallas_call(
            functools.partial(finish_kernel, src_count),
            out_shape=jax.ShapeDtypeStruct((src_count * LAGS * groups, LANES), jnp.float32),
            in_specs=[vmem] * 2,
            out_specs=vmem,
            scratch_shapes=[pltpu.VMEM(shape, jnp.float32)],
            compiler_params=pltpu.CompilerParams(vmem_limit_bytes=16 * 2**20),
            name="finish",
        )(near, chip)
        return total.reshape(1, src_count * LAGS, groups * LANES)[..., :channels]

    return jax.shard_map(
        body,
        mesh=mesh,
        in_specs=(P("chan", "win"), P("win"), P(), P("chan")),
        out_specs=P("win", None, "chan"),
        check_vma=False,
    )
```
